32 devices in a mesh: grp: 2 (over y), mode: 4 (over z), site: 4 (over x, core).
Axes of the slice: x: 2, y: 2, z: 4, core: 2. Of those that a mesh axis runs over, the one named last changes fastest.
Arguments:
- w_modes: bfloat16 [2, 1024, 12, 256], P(None, ('grp', 'mode'), None, 'site'), parts along dimension 1, may hold values from -6 to 6
- v_modes: bfloat16 [2, 512, 12, 256], P(None, ('grp', 'mode'), None, 'site'), parts along dimension 1, may hold values from -0.078125 to 0.078125
- momenta: int32 [4, 3], replicated, may hold values from -2 to 2
Outputs:
- meson: float32 [2, 4, 1024, 192], P(None, None, ('grp', 'mode', 'site')), parts along dimension 2
The draws below stay inside these ranges and needn't reach their ends.
There are 2 independent parts, one for each index of `grp`. The reference program is written for one: setup_inputs(seed, part) draws one part's arguments, and reference() takes and returns one part's arrays. A program takes and returns all parts, laid end to end along the dimension named above; an argument that names none is the same for every part. Nothing has to cross between parts.
All inputs are finite; a program needn't handle non-finite values.
Results may differ from the reference program's by a relative error of at most 0.0028.
Values may be sent and summed in bfloat16 or wider, within the bound.
A program may use at most 64 MiB of HBM per device.

```python
import jax
import jax.numpy as jnp
import numpy as np
from jax import lax

W_DEV = 128
VB = 64
NPH = 4
LAT = 96
STEPS = 1
NW = 512
NV = 256
SITES = 256


def with_ends(drawn, stream_key, low, top_value):
    spot = [jax.random.randint(jax.random.fold_in(stream_key, axis), (), 0, length) for axis, length in enumerate(drawn.shape)]
    main_axis = drawn.shape.index(max(drawn.shape))
    beside = spot[:main_axis] + [(spot[main_axis] + 1) % drawn.shape[main_axis]] + spot[main_axis + 1:]
    return drawn.at[tuple(spot)].set(low).at[tuple(beside)].set(top_value)


def shard_levels(own_key, extent, cuts, smallest, high):
    gain = 1.0
    for position, shards_of in cuts:
        steps = jax.random.uniform(jax.random.fold_in(jax.random.fold_in(own_key, 6), position), (shards_of,), jnp.float32, smallest / len(cuts), high / len(cuts))
        gain = gain * jnp.repeat(jnp.exp(steps), extent[position] // shards_of).reshape((-1,) + (1,) * (len(extent) - 1 - position))
    return gain


def noise(key, extent, deviation, limit, shards=(), kind=jnp.bfloat16):
    result = deviation * jax.random.normal(key, extent, jnp.float32)
    if shards:
        result = result * shard_levels(key, extent, shards, -0.22, 0.18)
    return jnp.clip(result, -limit, limit).astype(kind)


def setup_inputs(seed: int = 0, part: int = 0) -> dict:
    seeds = jax.random.split(jax.random.key(seed), 4)
    own_keys = jax.random.split(jax.random.fold_in(seeds[3], part), 4)
    w_modes = noise(own_keys[0], (2, NW, 12, SITES), 1.0, 6.0, ((1, 4), (3, 4)))
    v_modes = noise(own_keys[1], (2, NV, 12, SITES), (24 * SITES) ** -0.5, 0.078125, ((1, 4), (3, 4)))
    momenta = with_ends(jax.random.randint(seeds[2], (NPH, 3), -2, 3), jax.random.fold_in(seeds[2], 1), -2, 2).astype(jnp.int32)
    return {"w_modes": w_modes, "v_modes": v_modes, "momenta": momenta}


def make_phase(momenta, first, count):
    index = first + jnp.arange(count, dtype=jnp.int32)
    xcoord = index % LAT
    ycoord = (index // LAT) % LAT
    zcoord = index // (LAT * LAT)
    total = momenta[:, 0:1] * xcoord[None, :] + momenta[:, 1:2] * ycoord[None, :] + momenta[:, 2:3] * zcoord[None, :]
    wound = total % LAT
    angle = (-2.0 * np.pi / LAT) * wound.astype(jnp.float32)
    return jnp.cos(angle), jnp.sin(angle)


def apply_gamma(vectors):
    count = vectors.shape[1]
    sites = vectors.shape[3]
    shaped = vectors.reshape(2, count, 4, 3, sites)
    signs = jnp.array([-1.0, 1.0, 1.0, -1.0], jnp.float32)
    flipped = shaped[:, :, ::-1].astype(jnp.float32) * signs[None, None, :, None, None]
    return flipped.astype(jnp.bfloat16).reshape(2, count, 12, sites)


def phased_rows(wblock, cosine, sine):
    wreal = wblock[0].astype(jnp.float32)
    wimag = wblock[1].astype(jnp.float32)
    creal = cosine[:, None, None, :]
    cimag = sine[:, None, None, :]
    areal = wreal[None] * creal + wimag[None] * cimag
    aimag = wreal[None] * cimag - wimag[None] * creal
    rows = areal.shape[0] * areal.shape[1]
    width = areal.shape[2] * areal.shape[3]
    return jnp.concatenate([areal.reshape(rows, width), aimag.reshape(rows, width)], axis=0).astype(jnp.bfloat16)


def reference(w_modes, v_modes, momenta):
    nmode = w_modes.shape[1] // W_DEV
    sites = w_modes.shape[3]
    cosine, sine = make_phase(momenta, 0, sites)
    gv = apply_gamma(v_modes).reshape(2, nmode, VB, 12, sites)
    width = 12 * sites
    nblocks = 2 * STEPS + 1
    nband = nblocks * VB

    def one_owner(owner):
        wblock = lax.dynamic_slice_in_dim(w_modes, (owner * W_DEV).astype(jnp.int32), W_DEV, 1)
        lhs = phased_rows(wblock, cosine, sine).astype(jnp.float32)
        picks = ((owner + jnp.arange(nblocks, dtype=jnp.int32) - STEPS) % nmode).astype(jnp.int32)
        band = jnp.take(gv, picks, axis=1).reshape(2, nband, width)
        rhs = jnp.concatenate([band[0], band[1]], axis=0).astype(jnp.float32)
        prod = lax.dot_general(lhs, rhs, (((1,), (1,)), ((), ())), preferred_element_type=jnp.float32)
        half_rows = NPH * W_DEV
        real_part = prod[:half_rows, :nband] - prod[half_rows:, nband:]
        imag_part = prod[:half_rows, nband:] + prod[half_rows:, :nband]
        return jnp.stack([real_part, imag_part]).reshape(2, NPH, W_DEV, nband)

    owners = jnp.arange(nmode, dtype=jnp.int32)
    stacked = lax.map(one_owner, owners)
    return jnp.transpose(stacked, (1, 2, 0, 3, 4)).reshape(2, NPH, nmode * W_DEV, nband)
```

```python
import functools

import jax
import jax.numpy as jnp
import numpy as np
from jax import lax
from jax.experimental import pallas as pl
from jax.experimental.pallas import tpu as pltpu
from jax.sharding import PartitionSpec as P

LAT = 96
REACH = 4
SPINS = 4
SIGNS = (-1.0, 1.0, 1.0, -1.0)
MESH = pl.DeviceIdType.MESH


def phase_table(mom_ref, nph, rows, sites):
    shape = (sites, nph * rows)
    index = lax.axis_index("site") * sites + lax.broadcasted_iota(jnp.int32, shape, 0)
    lane = lax.broadcasted_iota(jnp.int32, shape, 1)
    lat = jnp.full(shape, LAT, jnp.int32)
    xcoord = lax.rem(index, lat)
    upper = lax.div(index, lat)
    ycoord = lax.rem(upper, lat)
    zcoord = lax.div(upper, lat)
    total = jnp.zeros(shape, jnp.int32)
    for p in range(nph):
        here = mom_ref[p, 0] * xcoord + mom_ref[p, 1] * ycoord + mom_ref[p, 2] * zcoord
        total = jnp.where((lane >= p * rows) & (lane < (p + 1) * rows), here, total)
    wound = lax.rem(total, lat)
    wound = jnp.where(wound < 0, wound + LAT, wound)
    angle = (-2.0 * np.pi / LAT) * wound.astype(jnp.float32)
    return jnp.cos(angle), jnp.sin(angle)


def kernel(
    nmode, nsite, reach,
    w_hbm, v_hbm, mom_ref, out_ref,
    w_ref, v_ref, packed, arrived, lhs, outgoing, incoming, total,
    load_sem, vsend_sem, vrecv_sem, psend_sem, precv_sem,
):
    mode = lax.axis_index("mode")
    site = lax.axis_index("site")
    _, nsc, sites, wrows = w_ref.shape
    nph = mom_ref.shape[0]
    rows = wrows // nsite
    half = nph * rows
    vrows = packed.shape[0]
    nblocks = 2 * reach + 1
    step = 1 - 2 * lax.rem(site, 2) if nsite % 2 == 0 else 1

    load_v = pltpu.make_async_copy(v_hbm, v_ref, load_sem.at[0])
    load_w = pltpu.make_async_copy(w_hbm, w_ref, load_sem.at[1])
    load_v.start()
    load_w.start()

    def mode_of(offset):
        return {"mode": lax.rem(mode + offset + nmode, nmode)}

    def site_of(distance):
        return lax.rem(site + step * distance + nsite, nsite)

    barrier = pltpu.get_barrier_semaphore()
    offsets = [o for o in range(-reach, reach + 1) if o != 0]
    for offset in offsets:
        pl.semaphore_signal(barrier, inc=1, device_id=mode_of(offset), device_id_type=MESH)
    for distance in range(1, nsite):
        pl.semaphore_signal(
            barrier, inc=1, device_id={"site": site_of(distance)}, device_id_type=MESH
        )

    load_v.wait()
    for sc in range(nsc):
        packed[:, sc * 2 * sites : (sc + 1) * 2 * sites] = jnp.concatenate(
            [v_ref[0, sc], v_ref[1, sc]], axis=1
        )
    pl.semaphore_wait(barrier, len(offsets) + nsite - 1)

    vcopies = []
    for far in range(1, reach + 1):
        for offset in (far, -far):
            slot = offset + reach
            copy = pltpu.make_async_remote_copy(
                src_ref=packed,
                dst_ref=arrived.at[slot],
                send_sem=vsend_sem.at[slot],
                recv_sem=vrecv_sem.at[slot],
                device_id=mode_of(-offset),
                device_id_type=MESH,
            )
            copy.start()
            vcopies.append(copy)

    cosine, sine = phase_table(mom_ref, nph, rows, sites)
    cosine = jnp.concatenate([cosine] * nsite, axis=1)
    sine = jnp.concatenate([sine] * nsite, axis=1)
    shape = (wrows, nsite * half)
    mode_row = lax.broadcasted_iota(jnp.int32, shape, 0)
    lane = lax.broadcasted_iota(jnp.int32, shape, 1)
    spread = jnp.zeros(shape, jnp.float32)
    for piece in range(nsite * nph):
        source = lane - piece * rows + (piece // nph) * rows
        inside = (lane >= piece * rows) & (lane < (piece + 1) * rows)
        spread = jnp.where(inside & (mode_row == source), 1.0, spread)
    spread = spread.astype(jnp.bfloat16)

    load_w.wait()
    colours = nsc // SPINS
    for sc in range(nsc):
        spin, colour = sc // colours, sc % colours
        sign = SIGNS[spin]
        source = colours * (SPINS - 1 - spin) + colour
        wreal = jnp.dot(w_ref[0, source], spread, preferred_element_type=jnp.float32)
        wimag = jnp.dot(w_ref[1, source], spread, preferred_element_type=jnp.float32)
        areal = (sign * (wreal * cosine + wimag * sine)).astype(jnp.bfloat16)
        aimag = (sign * (wreal * sine - wimag * cosine)).astype(jnp.bfloat16)
        top = pl.ds(sc * 2 * sites, sites)
        low = pl.ds(sc * 2 * sites + sites, sites)
        for s in range(nsite):
            part = slice(s * half, (s + 1) * half)
            lhs[s, top, 0:half] = areal[:, part]
            lhs[s, top, half : 2 * half] = aimag[:, part]
            lhs[s, low, 0:half] = -aimag[:, part]
            lhs[s, low, half : 2 * half] = areal[:, part]

    distances = list(range(nsite - 1, 0, -1))
    if nsite > 2:
        distances.remove(nsite // 2)
        distances.insert(0, nsite // 2)

    def partial_copy(slot, distance):
        return pltpu.make_async_remote_copy(
            src_ref=outgoing.at[slot, distance - 1],
            dst_ref=incoming.at[slot, distance - 1],
            send_sem=psend_sem.at[slot, distance - 1],
            recv_sem=precv_sem.at[slot, distance - 1],
            device_id={"site": site_of(distance)},
            device_id_type=MESH,
        )

    def handle(block, slot):
        for distance in distances:
            outgoing[slot, distance - 1] = jnp.dot(
                block, lhs[site_of(distance)], preferred_element_type=jnp.float32
            ).astype(jnp.bfloat16)
            partial_copy(slot, distance).start()
        total[slot] = jnp.dot(block, lhs[site], preferred_element_type=jnp.float32)

    handle(packed[...], reach)
    first = jnp.where(2 * mode < nmode, 1, -1)
    for far in range(1, reach + 1):
        for direction in (first, -first):
            slot = reach + direction * far
            pltpu.make_async_remote_copy(
                src_ref=packed,
                dst_ref=arrived.at[slot],
                send_sem=vsend_sem.at[slot],
                recv_sem=vrecv_sem.at[slot],
                device_id=mode_of(-1),
                device_id_type=MESH,
            ).wait_recv()
            handle(arrived[slot], slot)

    for slot in range(nblocks):
        value = total[slot]
        for distance in distances:
            partial_copy(slot, distance).wait_recv()
            value = value + incoming[slot, distance - 1].astype(jnp.float32)
        out_ref[:, slot * vrows : (slot + 1) * vrows] = value.T
    for copy in vcopies:
        copy.wait_send()
    for slot in range(nblocks):
        for distance in distances:
            partial_copy(slot, distance).wait_send()


def shards(nmode, nsite, w_modes, v_modes, momenta):
    _, wrows, nsc, sites = w_modes.shape
    vrows = v_modes.shape[1]
    nph = momenta.shape[0]
    reach = min(REACH, (nmode - 1) // 2)
    nblocks = 2 * reach + 1
    rows = wrows // nsite
    width = 2 * nsc * sites
    lanes = 2 * nph * rows
    out = pl.pallas_call(
        functools.partial(kernel, nmode, nsite, reach),
        out_shape=jax.ShapeDtypeStruct((lanes, nblocks * vrows), jnp.float32),
        in_specs=[
            pl.BlockSpec(memory_space=pl.ANY),
            pl.BlockSpec(memory_space=pl.ANY),
            pl.BlockSpec(memory_space=pltpu.SMEM),
        ],
        out_specs=pl.BlockSpec(memory_space=pltpu.VMEM),
        scratch_shapes=[
            pltpu.VMEM((2, nsc, sites, wrows), jnp.bfloat16),
            pltpu.VMEM((2, nsc, vrows, sites), jnp.bfloat16),
            pltpu.VMEM((vrows, width), jnp.bfloat16),
            pltpu.VMEM((nblocks, vrows, width), jnp.bfloat16),
            pltpu.VMEM((nsite, width, lanes), jnp.bfloat16),
            pltpu.VMEM((nblocks, nsite - 1, vrows, lanes), jnp.bfloat16),
            pltpu.VMEM((nblocks, nsite - 1, vrows, lanes), jnp.bfloat16),
            pltpu.VMEM((nblocks, vrows, lanes), jnp.float32),
            pltpu.SemaphoreType.DMA((2,)),
            pltpu.SemaphoreType.DMA((nblocks,)),
            pltpu.SemaphoreType.DMA((nblocks,)),
            pltpu.SemaphoreType.DMA((nblocks, nsite - 1)),
            pltpu.SemaphoreType.DMA((nblocks, nsite - 1)),
        ],
        compiler_params=pltpu.CompilerParams(
            collective_id=0, has_side_effects=True, vmem_limit_bytes=40 * 1024 * 1024
        ),
    )(jnp.transpose(w_modes, (0, 2, 3, 1)), jnp.transpose(v_modes, (0, 2, 1, 3)), momenta)
    return out.reshape(2, nph, rows, nblocks * vrows)


def solution(mesh):
    placed = (P(None, ("grp", "mode"), None, "site"), P(None, ("grp", "mode"), None, "site"), P())
    return jax.shard_map(
        functools.partial(shards, mesh.shape["mode"], mesh.shape["site"]),
        mesh=mesh,
        in_specs=placed,
        out_specs=P(None, None, ("grp", "mode", "site"), None),
        check_vma=False,
    )
```

```python
import functools

import jax
import jax.numpy as jnp
import numpy as np
from jax import lax
from jax.experimental import pallas as pl
from jax.experimental.pallas import tpu as pltpu
from jax.sharding import PartitionSpec as P

LAT = 96
REACH = 4
SPINS = 4
PIECES = 2
SIGNS = (-1.0, 1.0, 1.0, -1.0)
MESH = pl.DeviceIdType.MESH


def phase_table(mom_ref, nph, rows, sites):
    shape = (sites, nph * rows)
    index = lax.axis_index("site") * sites + lax.broadcasted_iota(jnp.int32, shape, 0)
    lane = lax.broadcasted_iota(jnp.int32, shape, 1)
    lat = jnp.full(shape, LAT, jnp.int32)
    xcoord = lax.rem(index, lat)
    upper = lax.div(index, lat)
    ycoord = lax.rem(upper, lat)
    zcoord = lax.div(upper, lat)
    total = jnp.zeros(shape, jnp.int32)
    for p in range(nph):
        here = mom_ref[p, 0] * xcoord + mom_ref[p, 1] * ycoord + mom_ref[p, 2] * zcoord
        total = jnp.where((lane >= p * rows) & (lane < (p + 1) * rows), here, total)
    wound = lax.rem(total, lat)
    wound = jnp.where(wound < 0, wound + LAT, wound)
    angle = (-2.0 * np.pi / LAT) * wound.astype(jnp.float32)
    return jnp.cos(angle), jnp.sin(angle)


def kernel(
    nmode, nsite, reach,
    w_hbm, v_hbm, mom_hbm, out_ref,
    w_ref, v_ref, mom_ref, packed, arrived, lhs, outgoing, incoming, total,
    load_sem, vsend_sem, vrecv_sem, psend_sem, precv_sem,
):
    mode = lax.axis_index("mode")
    site = lax.axis_index("site")
    _, nsc, sites, wrows = w_ref.shape
    nph = mom_ref.shape[0]
    rows = wrows // nsite
    half = nph * rows
    npiece, prows, _ = packed.shape
    vrows = npiece * prows
    nblocks = 2 * reach + 1
    step = 1 - 2 * lax.rem(site, 2) if nsite % 2 == 0 else 1

    load_v = pltpu.make_async_copy(v_hbm, v_ref, load_sem.at[0])
    load_w = pltpu.make_async_copy(w_hbm, w_ref, load_sem.at[1])
    load_mom = pltpu.make_async_copy(mom_hbm, mom_ref, load_sem.at[2])
    load_v.start()
    load_mom.start()
    load_w.start()

    def mode_of(offset):
        return {"mode": lax.rem(mode + offset + nmode, nmode)}

    def site_of(distance):
        return lax.rem(site + step * distance + nsite, nsite)

    barrier = pltpu.get_barrier_semaphore()
    offsets = [o for o in range(-reach, reach + 1) if o != 0]
    for offset in offsets:
        pl.semaphore_signal(barrier, inc=1, device_id=mode_of(offset), device_id_type=MESH)
    for distance in range(1, nsite):
        pl.semaphore_signal(
            barrier, inc=1, device_id={"site": site_of(distance)}, device_id_type=MESH
        )

    load_v.wait()
    for piece in range(npiece):
        taken = slice(piece * prows, (piece + 1) * prows)
        for sc in range(nsc):
            packed[piece, :, sc * 2 * sites : (sc + 1) * 2 * sites] = jnp.concatenate(
                [v_ref[0, sc, taken], v_ref[1, sc, taken]], axis=1
            )
    pl.semaphore_wait(barrier, len(offsets) + nsite - 1)

    def vcopy(offset, piece):
        slot = offset + reach
        return pltpu.make_async_remote_copy(
            src_ref=packed.at[piece],
            dst_ref=arrived.at[slot, piece],
            send_sem=vsend_sem.at[slot, piece],
            recv_sem=vrecv_sem.at[slot, piece],
            device_id=mode_of(-offset),
            device_id_type=MESH,
        )

    toward = jnp.where(2 * mode < nmode, 1, -1)
    order = [toward * far for far in range(1, reach + 1)]
    order = [side * offset for offset in order for side in (1, -1)]
    for offset in order:
        for piece in range(npiece):
            vcopy(offset, piece).start()

    load_mom.wait()
    cosine, sine = phase_table(mom_ref, nph, rows, sites)
    cosine = jnp.concatenate([cosine] * nsite, axis=1)
    sine = jnp.concatenate([sine] * nsite, axis=1)
    shape = (wrows, nsite * half)
    mode_row = lax.broadcasted_iota(jnp.int32, shape, 0)
    lane = lax.broadcasted_iota(jnp.int32, shape, 1)
    spread = jnp.zeros(shape, jnp.float32)
    for piece in range(nsite * nph):
        source = lane - piece * rows + (piece // nph) * rows
        inside = (lane >= piece * rows) & (lane < (piece + 1) * rows)
        spread = jnp.where(inside & (mode_row == source), 1.0, spread)
    spread = spread.astype(jnp.bfloat16)

    load_w.wait()
    colours = nsc // SPINS
    for sc in range(nsc):
        spin, colour = sc // colours, sc % colours
        sign = SIGNS[spin]
        source = colours * (SPINS - 1 - spin) + colour
        wreal = jnp.dot(w_ref[0, source], spread, preferred_element_type=jnp.float32)
        wimag = jnp.dot(w_ref[1, source], spread, preferred_element_type=jnp.float32)
        areal = (sign * (wreal * cosine + wimag * sine)).astype(jnp.bfloat16)
        aimag = (sign * (wreal * sine - wimag * cosine)).astype(jnp.bfloat16)
        top = pl.ds(sc * 2 * sites, sites)
        low = pl.ds(sc * 2 * sites + sites, sites)
        for s in range(nsite):
            part = slice(s * half, (s + 1) * half)
            lhs[s, top, 0:half] = areal[:, part]
            lhs[s, top, half : 2 * half] = aimag[:, part]
            lhs[s, low, 0:half] = -aimag[:, part]
            lhs[s, low, half : 2 * half] = areal[:, part]

    distances = list(range(nsite - 1, 0, -1))
    if nsite > 2:
        distances.remove(nsite // 2)
        distances.insert(0, nsite // 2)

    def partial_copy(slot, piece, distance):
        return pltpu.make_async_remote_copy(
            src_ref=outgoing.at[slot, piece, distance - 1],
            dst_ref=incoming.at[slot, piece, distance - 1],
            send_sem=psend_sem.at[slot, piece, distance - 1],
            recv_sem=precv_sem.at[slot, piece, distance - 1],
            device_id={"site": site_of(distance)},
            device_id_type=MESH,
        )

    def handle(block, slot, piece):
        for distance in distances:
            outgoing[slot, piece, distance - 1] = jnp.dot(
                block, lhs[site_of(distance)], preferred_element_type=jnp.float32
            ).astype(jnp.bfloat16)
            partial_copy(slot, piece, distance).start()
        total[slot, piece] = jnp.dot(block, lhs[site], preferred_element_type=jnp.float32)

    for piece in range(npiece):
        handle(packed[piece], reach, piece)
    for offset in order:
        for piece in range(npiece):
            vcopy(offset, piece).wait_recv()
            handle(arrived[offset + reach, piece], offset + reach, piece)

    for slot in range(nblocks):
        for piece in range(npiece):
            value = total[slot, piece]
            for distance in distances:
                partial_copy(slot, piece, distance).wait_recv()
                value = value + incoming[slot, piece, distance - 1].astype(jnp.float32)
            total[slot, piece] = value
    out_ref[...] = total[...].reshape(nblocks * vrows, 2 * half).T
    for offset in order:
        for piece in range(npiece):
            vcopy(offset, piece).wait_send()
    for slot in range(nblocks):
        for piece in range(npiece):
            for distance in distances:
                partial_copy(slot, piece, distance).wait_send()


def shards(nmode, nsite, w_modes, v_modes, momenta):
    _, wrows, nsc, sites = w_modes.shape
    vrows = v_modes.shape[1]
    nph = momenta.shape[0]
    reach = min(REACH, (nmode - 1) // 2)
    nblocks = 2 * reach + 1
    rows = wrows // nsite
    width = 2 * nsc * sites
    lanes = 2 * nph * rows
    prows = vrows // PIECES
    out = pl.pallas_call(
        functools.partial(kernel, nmode, nsite, reach),
        out_shape=jax.ShapeDtypeStruct((lanes, nblocks * vrows), jnp.float32),
        in_specs=[
            pl.BlockSpec(memory_space=pl.ANY),
            pl.BlockSpec(memory_space=pl.ANY),
            pl.BlockSpec(memory_space=pl.ANY),
        ],
        out_specs=pl.BlockSpec(memory_space=pltpu.VMEM),
        scratch_shapes=[
            pltpu.VMEM((2, nsc, sites, wrows), jnp.bfloat16),
            pltpu.VMEM((2, nsc, vrows, sites), jnp.bfloat16),
            pltpu.SMEM((nph, 3), jnp.int32),
            pltpu.VMEM((PIECES, prows, width), jnp.bfloat16),
            pltpu.VMEM((nblocks, PIECES, prows, width), jnp.bfloat16),
            pltpu.VMEM((nsite, width, lanes), jnp.bfloat16),
            pltpu.VMEM((nblocks, PIECES, nsite - 1, prows, lanes), jnp.bfloat16),
            pltpu.VMEM((nblocks, PIECES, nsite - 1, prows, lanes), jnp.bfloat16),
            pltpu.VMEM((nblocks, PIECES, prows, lanes), jnp.float32),
            pltpu.SemaphoreType.DMA((3,)),
            pltpu.SemaphoreType.DMA((nblocks, PIECES)),
            pltpu.SemaphoreType.DMA((nblocks, PIECES)),
            pltpu.SemaphoreType.DMA((nblocks, PIECES, nsite - 1)),
            pltpu.SemaphoreType.DMA((nblocks, PIECES, nsite - 1)),
        ],
        compiler_params=pltpu.CompilerParams(
            collective_id=0, has_side_effects=True, vmem_limit_bytes=60 * 1024 * 1024
        ),
    )(jnp.transpose(w_modes, (0, 2, 3, 1)), jnp.transpose(v_modes, (0, 2, 1, 3)), momenta)
    return out.reshape(2, nph, rows, nblocks * vrows)


def solution(mesh):
    placed = (P(None, ("grp", "mode"), None, "site"), P(None, ("grp", "mode"), None, "site"), P())
    return jax.shard_map(
        functools.partial(shards, mesh.shape["mode"], mesh.shape["site"]),
        mesh=mesh,
        in_specs=placed,
        out_specs=P(None, None, ("grp", "mode", "site"), None),
        check_vma=False,
    )
```

```python
import functools

import jax
import jax.numpy as jnp
import numpy as np
from jax import lax
from jax.experimental import pallas as pl
from jax.experimental.pallas import tpu as pltpu
from jax.sharding import PartitionSpec as P

LAT = 96
REACH = 4
SPINS = 4
PIECES = 2
SIGNS = (-1.0, 1.0, 1.0, -1.0)
MESH = pl.DeviceIdType.MESH


def phase_table(mom_ref, nph, rows, sites):
    shape = (sites, nph * rows)
    index = lax.axis_index("site") * sites + lax.broadcasted_iota(jnp.int32, shape, 0)
    lane = lax.broadcasted_iota(jnp.int32, shape, 1)
    lat = jnp.full(shape, LAT, jnp.int32)
    xcoord = lax.rem(index, lat)
    upper = lax.div(index, lat)
    ycoord = lax.rem(upper, lat)
    zcoord = lax.div(upper, lat)
    total = jnp.zeros(shape, jnp.int32)
    for p in range(nph):
        here = mom_ref[p, 0] * xcoord + mom_ref[p, 1] * ycoord + mom_ref[p, 2] * zcoord
        total = jnp.where((lane >= p * rows) & (lane < (p + 1) * rows), here, total)
    wound = lax.rem(total, lat)
    wound = jnp.where(wound < 0, wound + LAT, wound)
    angle = (-2.0 * np.pi / LAT) * wound.astype(jnp.float32)
    return jnp.cos(angle), jnp.sin(angle)


def kernel(
    nmode, nsite, reach,
    w_hbm, v_hbm, mom_hbm, out_ref,
    w_ref, v_ref, mom_ref, packed, arrived, lhs, outgoing, incoming, total,
    load_sem, vsend_sem, vrecv_sem, psend_sem, precv_sem,
):
    mode = lax.axis_index("mode")
    site = lax.axis_index("site")
    _, nsc, sites, wrows = w_ref.shape
    nph = mom_ref.shape[0]
    rows = wrows // nsite
    half = nph * rows
    npiece, prows, _ = packed.shape
    vrows = npiece * prows
    nblocks = 2 * reach + 1
    step = 1 - 2 * lax.rem(site, 2) if nsite % 2 == 0 else 1

    def load_v(piece):
        return pltpu.make_async_copy(
            v_hbm.at[:, :, pl.ds(piece * prows, prows), :], v_ref.at[piece], load_sem.at[2 + piece]
        )

    for piece in range(npiece):
        load_v(piece).start()
    load_w = pltpu.make_async_copy(w_hbm, w_ref, load_sem.at[0])
    load_mom = pltpu.make_async_copy(mom_hbm, mom_ref, load_sem.at[1])
    load_mom.start()
    load_w.start()

    def mode_of(offset):
        return {"mode": lax.rem(mode + offset + nmode, nmode)}

    def site_of(distance):
        return lax.rem(site + step * distance + nsite, nsite)

    barrier = pltpu.get_barrier_semaphore()
    offsets = [o for o in range(-reach, reach + 1) if o != 0]
    for offset in offsets:
        pl.semaphore_signal(barrier, inc=1, device_id=mode_of(offset), device_id_type=MESH)
    for distance in range(1, nsite):
        pl.semaphore_signal(
            barrier, inc=1, device_id={"site": site_of(distance)}, device_id_type=MESH
        )

    def vcopy(offset, piece):
        slot = offset + reach
        return pltpu.make_async_remote_copy(
            src_ref=packed.at[piece],
            dst_ref=arrived.at[slot, piece],
            send_sem=vsend_sem.at[slot, piece],
            recv_sem=vrecv_sem.at[slot, piece],
            device_id=mode_of(-offset),
            device_id_type=MESH,
        )

    toward = jnp.where(2 * mode < nmode, 1, -1)
    order = [toward * far for far in range(1, reach + 1)]
    order = [side * offset for offset in order for side in (1, -1)]
    for piece in range(npiece):
        load_v(piece).wait()
        for sc in range(nsc):
            packed[piece, :, sc * 2 * sites : (sc + 1) * 2 * sites] = jnp.concatenate(
                [v_ref[piece, 0, sc], v_ref[piece, 1, sc]], axis=1
            )
        if piece == 0:
            pl.semaphore_wait(barrier, len(offsets) + nsite - 1)
        vcopy(order[0], piece).start()
    for offset in order[1:]:
        for piece in range(npiece):
            vcopy(offset, piece).start()

    load_mom.wait()
    cosine, sine = phase_table(mom_ref, nph, rows, sites)
    cosine = jnp.concatenate([cosine] * nsite, axis=1)
    sine = jnp.concatenate([sine] * nsite, axis=1)
    shape = (wrows, nsite * half)
    mode_row = lax.broadcasted_iota(jnp.int32, shape, 0)
    lane = lax.broadcasted_iota(jnp.int32, shape, 1)
    spread = jnp.zeros(shape, jnp.float32)
    for piece in range(nsite * nph):
        source = lane - piece * rows + (piece // nph) * rows
        inside = (lane >= piece * rows) & (lane < (piece + 1) * rows)
        spread = jnp.where(inside & (mode_row == source), 1.0, spread)
    spread = spread.astype(jnp.bfloat16)

    load_w.wait()
    colours = nsc // SPINS
    for sc in range(nsc):
        spin, colour = sc // colours, sc % colours
        sign = SIGNS[spin]
        source = colours * (SPINS - 1 - spin) + colour
        wreal = jnp.dot(w_ref[0, source], spread, preferred_element_type=jnp.float32)
        wimag = jnp.dot(w_ref[1, source], spread, preferred_element_type=jnp.float32)
        areal = (sign * (wreal * cosine + wimag * sine)).astype(jnp.bfloat16)
        aimag = (sign * (wreal * sine - wimag * cosine)).astype(jnp.bfloat16)
        top = pl.ds(sc * 2 * sites, sites)
        low = pl.ds(sc * 2 * sites + sites, sites)
        for s in range(nsite):
            part = slice(s * half, (s + 1) * half)
            lhs[s, top, 0:half] = areal[:, part]
            lhs[s, top, half : 2 * half] = aimag[:, part]
            lhs[s, low, 0:half] = -aimag[:, part]
            lhs[s, low, half : 2 * half] = areal[:, part]

    distances = list(range(nsite - 1, 0, -1))
    if nsite > 2:
        distances.remove(nsite // 2)
        distances.insert(0, nsite // 2)

    def partial_copy(slot, piece, distance):
        return pltpu.make_async_remote_copy(
            src_ref=outgoing.at[slot, piece, distance - 1],
            dst_ref=incoming.at[slot, piece, distance - 1],
            send_sem=psend_sem.at[slot, piece, distance - 1],
            recv_sem=precv_sem.at[slot, piece, distance - 1],
            device_id={"site": site_of(distance)},
            device_id_type=MESH,
        )

    def handle(block, slot, piece):
        for distance in distances:
            outgoing[slot, piece, distance - 1] = jnp.dot(
                block, lhs[site_of(distance)], preferred_element_type=jnp.float32
            ).astype(jnp.bfloat16)
            partial_copy(slot, piece, distance).start()
        total[slot, piece] = jnp.dot(block, lhs[site], preferred_element_type=jnp.float32)

    for piece in range(npiece):
        handle(packed[piece], reach, piece)
    for offset in order:
        for piece in range(npiece):
            vcopy(offset, piece).wait_recv()
            handle(arrived[offset + reach, piece], offset + reach, piece)

    for slot in range(nblocks):
        for piece in range(npiece):
            value = total[slot, piece]
            for distance in distances:
                partial_copy(slot, piece, distance).wait_recv()
                value = value + incoming[slot, piece, distance - 1].astype(jnp.float32)
            total[slot, piece] = value
    out_ref[...] = total[...].reshape(nblocks * vrows, 2 * half).T
    for offset in order:
        for piece in range(npiece):
            vcopy(offset, piece).wait_send()
    for slot in range(nblocks):
        for piece in range(npiece):
            for distance in distances:
                partial_copy(slot, piece, distance).wait_send()


def shards(nmode, nsite, w_modes, v_modes, momenta):
    _, wrows, nsc, sites = w_modes.shape
    vrows = v_modes.shape[1]
    nph = momenta.shape[0]
    reach = min(REACH, (nmode - 1) // 2)
    nblocks = 2 * reach + 1
    rows = wrows // nsite
    width = 2 * nsc * sites
    lanes = 2 * nph * rows
    prows = vrows // PIECES
    out = pl.pallas_call(
        functools.partial(kernel, nmode, nsite, reach),
        out_shape=jax.ShapeDtypeStruct((lanes, nblocks * vrows), jnp.float32),
        in_specs=[
            pl.BlockSpec(memory_space=pltpu.HBM),
            pl.BlockSpec(memory_space=pltpu.HBM),
            pl.BlockSpec(memory_space=pltpu.HBM),
        ],
        out_specs=pl.BlockSpec(memory_space=pltpu.VMEM),
        scratch_shapes=[
            pltpu.VMEM((2, nsc, sites, wrows), jnp.bfloat16),
            pltpu.VMEM((PIECES, 2, nsc, prows, sites), jnp.bfloat16),
            pltpu.SMEM((nph, 3), jnp.int32),
            pltpu.VMEM((PIECES, prows, width), jnp.bfloat16),
            pltpu.VMEM((nblocks, PIECES, prows, width), jnp.bfloat16),
            pltpu.VMEM((nsite, width, lanes), jnp.bfloat16),
            pltpu.VMEM((nblocks, PIECES, nsite - 1, prows, lanes), jnp.bfloat16),
            pltpu.VMEM((nblocks, PIECES, nsite - 1, prows, lanes), jnp.bfloat16),
            pltpu.VMEM((nblocks, PIECES, prows, lanes), jnp.float32),
            pltpu.SemaphoreType.DMA((2 + PIECES,)),
            pltpu.SemaphoreType.DMA((nblocks, PIECES)),
            pltpu.SemaphoreType.DMA((nblocks, PIECES)),
            pltpu.SemaphoreType.DMA((nblocks, PIECES, nsite - 1)),
            pltpu.SemaphoreType.DMA((nblocks, PIECES, nsite - 1)),
        ],
        compiler_params=pltpu.CompilerParams(
            collective_id=0, has_side_effects=True, vmem_limit_bytes=32 * 1024 * 1024
        ),
    )(
        pltpu.with_memory_space_constraint(jnp.transpose(w_modes, (0, 2, 3, 1)), pltpu.HBM),
        pltpu.with_memory_space_constraint(jnp.transpose(v_modes, (0, 2, 1, 3)), pltpu.HBM),
        pltpu.with_memory_space_constraint(momenta, pltpu.HBM),
    )
    return out.reshape(2, nph, rows, nblocks * vrows)


def solution(mesh):
    placed = (P(None, ("grp", "mode"), None, "site"), P(None, ("grp", "mode"), None, "site"), P())
    return jax.shard_map(
        functools.partial(shards, mesh.shape["mode"], mesh.shape["site"]),
        mesh=mesh,
        in_specs=placed,
        out_specs=P(None, None, ("grp", "mode", "site"), None),
        check_vma=False,
    )
```

```python
import functools

import jax
import jax.numpy as jnp
import numpy as np
from jax import lax
from jax.experimental import pallas as pl
from jax.experimental.pallas import tpu as pltpu
from jax.sharding import PartitionSpec as P

LAT = 96
REACH = 4
SPINS = 4
PIECES = 2
SIGNS = (-1.0, 1.0, 1.0, -1.0)
MESH = pl.DeviceIdType.MESH


def phase_table(mom_ref, nph, rows, sites):
    shape = (sites, nph * rows)
    index = lax.axis_index("site") * sites + lax.broadcasted_iota(jnp.int32, shape, 0)
    lane = lax.broadcasted_iota(jnp.int32, shape, 1)
    lat = jnp.full(shape, LAT, jnp.int32)
    xcoord = lax.rem(index, lat)
    upper = lax.div(index, lat)
    ycoord = lax.rem(upper, lat)
    zcoord = lax.div(upper, lat)
    total = jnp.zeros(shape, jnp.int32)
    for p in range(nph):
        here = mom_ref[p, 0] * xcoord + mom_ref[p, 1] * ycoord + mom_ref[p, 2] * zcoord
        total = jnp.where((lane >= p * rows) & (lane < (p + 1) * rows), here, total)
    wound = lax.rem(total, lat)
    wound = jnp.where(wound < 0, wound + LAT, wound)
    angle = (-2.0 * np.pi / LAT) * wound.astype(jnp.float32)
    return jnp.cos(angle), jnp.sin(angle)


def kernel(
    nmode, nsite, reach,
    w_hbm, v_hbm, mom_hbm, out_ref,
    w_ref, v_ref, mom_ref, packed, arrived, lhs, total,
    own_out, band_out, own_in, band_in,
    load_sem, vsend_sem, vrecv_sem, psend_sem, precv_sem,
):
    mode = lax.axis_index("mode")
    site = lax.axis_index("site")
    _, nsc, sites, wrows = w_ref.shape
    nph = mom_ref.shape[0]
    rows = wrows // nsite
    half = nph * rows
    npiece, prows, _ = packed.shape
    vrows = npiece * prows
    outgoing = [own_out] + [band_out.at[piece] for piece in range(npiece)]
    incoming = [own_in] + [band_in.at[piece] for piece in range(npiece)]
    step = 1 - 2 * lax.rem(site, 2) if nsite % 2 == 0 else 1

    def load_v(piece):
        return pltpu.make_async_copy(
            v_hbm.at[:, :, pl.ds(piece * prows, prows), :], v_ref.at[piece], load_sem.at[2 + piece]
        )

    for piece in range(npiece):
        load_v(piece).start()
    load_w = pltpu.make_async_copy(w_hbm, w_ref, load_sem.at[0])
    load_mom = pltpu.make_async_copy(mom_hbm, mom_ref, load_sem.at[1])
    load_mom.start()
    load_w.start()

    def mode_of(offset):
        return {"mode": lax.rem(mode + offset + nmode, nmode)}

    def site_of(distance):
        return lax.rem(site + step * distance + nsite, nsite)

    barrier = pltpu.get_barrier_semaphore()
    offsets = [o for o in range(-reach, reach + 1) if o != 0]
    for offset in offsets:
        pl.semaphore_signal(barrier, inc=1, device_id=mode_of(offset), device_id_type=MESH)
    for distance in range(1, nsite):
        pl.semaphore_signal(
            barrier, inc=1, device_id={"site": site_of(distance)}, device_id_type=MESH
        )

    def vcopy(piece, index):
        return pltpu.make_async_remote_copy(
            src_ref=packed.at[piece],
            dst_ref=arrived.at[piece, index],
            send_sem=vsend_sem.at[piece, index],
            recv_sem=vrecv_sem.at[piece, index],
            device_id=mode_of(-offsets[index]),
            device_id_type=MESH,
        )

    for piece in range(npiece):
        load_v(piece).wait()
        for sc in range(nsc):
            packed[piece, :, sc * 2 * sites : (sc + 1) * 2 * sites] = jnp.concatenate(
                [v_ref[piece, 0, sc], v_ref[piece, 1, sc]], axis=1
            )
        if piece == 0:
            pl.semaphore_wait(barrier, len(offsets) + nsite - 1)
            for index in range(len(offsets)):
                vcopy(piece, index).start()

    load_mom.wait()
    cosine, sine = phase_table(mom_ref, nph, rows, sites)
    cosine = jnp.concatenate([cosine] * nsite, axis=1)
    sine = jnp.concatenate([sine] * nsite, axis=1)
    shape = (wrows, nsite * half)
    mode_row = lax.broadcasted_iota(jnp.int32, shape, 0)
    lane = lax.broadcasted_iota(jnp.int32, shape, 1)
    spread = jnp.zeros(shape, jnp.float32)
    for piece in range(nsite * nph):
        source = lane - piece * rows + (piece // nph) * rows
        inside = (lane >= piece * rows) & (lane < (piece + 1) * rows)
        spread = jnp.where(inside & (mode_row == source), 1.0, spread)
    spread = spread.astype(jnp.bfloat16)

    load_w.wait()
    colours = nsc // SPINS
    for sc in range(nsc):
        spin, colour = sc // colours, sc % colours
        sign = SIGNS[spin]
        source = colours * (SPINS - 1 - spin) + colour
        wreal = jnp.dot(w_ref[0, source], spread, preferred_element_type=jnp.float32)
        wimag = jnp.dot(w_ref[1, source], spread, preferred_element_type=jnp.float32)
        areal = (sign * (wreal * cosine + wimag * sine)).astype(jnp.bfloat16)
        aimag = (sign * (wreal * sine - wimag * cosine)).astype(jnp.bfloat16)
        top = pl.ds(sc * 2 * sites, sites)
        low = pl.ds(sc * 2 * sites + sites, sites)
        for s in range(nsite):
            part = slice(s * half, (s + 1) * half)
            lhs[s, top, 0:half] = areal[:, part]
            lhs[s, top, half : 2 * half] = aimag[:, part]
            lhs[s, low, 0:half] = -aimag[:, part]
            lhs[s, low, half : 2 * half] = areal[:, part]

    distances = list(range(nsite - 1, 0, -1))
    if nsite > 2:
        distances.remove(nsite // 2)
        distances.insert(0, nsite // 2)

    def partial_copy(group, distance):
        return pltpu.make_async_remote_copy(
            src_ref=outgoing[group].at[distance - 1],
            dst_ref=incoming[group].at[distance - 1],
            send_sem=psend_sem.at[group, distance - 1],
            recv_sem=precv_sem.at[group, distance - 1],
            device_id={"site": site_of(distance)},
            device_id_type=MESH,
        )

    def handle(group, block):
        for distance in distances:
            outgoing[group][distance - 1] = jnp.dot(
                block, lhs[site_of(distance)], preferred_element_type=jnp.float32
            ).astype(jnp.bfloat16)
            partial_copy(group, distance).start()
        own = jnp.dot(block, lhs[site], preferred_element_type=jnp.float32)
        for start, stop, column in places(group):
            total[column : column + stop - start, :] = own[start:stop]

    def places(group):
        if group == 0:
            return [(0, vrows, reach * vrows)]
        return [
            (i * prows, (i + 1) * prows, (o + reach) * vrows + (group - 1) * prows)
            for i, o in enumerate(offsets)
        ]

    def gather(group):
        for distance in distances:
            partial_copy(group, distance).wait_recv()
        for start, stop, column in places(group):
            value = total[column : column + stop - start, :]
            for distance in distances:
                value = value + incoming[group][distance - 1, start:stop].astype(jnp.float32)
            total[column : column + stop - start, :] = value

    def next_pieces(piece):
        for index in range(len(offsets)):
            vcopy(piece - 1, index).wait_send()
            vcopy(piece, index).start()

    next_pieces(1)
    handle(0, packed[...].reshape(vrows, -1))
    for piece in range(npiece):
        if 1 <= piece < npiece - 1:
            next_pieces(piece + 1)
        for index in range(len(offsets)):
            vcopy(piece, index).wait_recv()
        handle(piece + 1, arrived[piece].reshape(len(offsets) * prows, -1))
        gather(piece)
    gather(npiece)
    out_ref[...] = total[...].T
    for index in range(len(offsets)):
        vcopy(npiece - 1, index).wait_send()
    for group in range(npiece + 1):
        for distance in distances:
            partial_copy(group, distance).wait_send()


def shards(nmode, nsite, w_modes, v_modes, momenta):
    _, wrows, nsc, sites = w_modes.shape
    vrows = v_modes.shape[1]
    nph = momenta.shape[0]
    reach = min(REACH, (nmode - 1) // 2)
    nblocks = 2 * reach + 1
    rows = wrows // nsite
    width = 2 * nsc * sites
    lanes = 2 * nph * rows
    prows = vrows // PIECES
    out = pl.pallas_call(
        functools.partial(kernel, nmode, nsite, reach),
        out_shape=jax.ShapeDtypeStruct((lanes, nblocks * vrows), jnp.float32),
        in_specs=[
            pl.BlockSpec(memory_space=pltpu.HBM),
            pl.BlockSpec(memory_space=pltpu.HBM),
            pl.BlockSpec(memory_space=pltpu.HBM),
        ],
        out_specs=pl.BlockSpec(memory_space=pltpu.VMEM),
        scratch_shapes=[
            pltpu.VMEM((2, nsc, sites, wrows), jnp.bfloat16),
            pltpu.VMEM((PIECES, 2, nsc, prows, sites), jnp.bfloat16),
            pltpu.SMEM((nph, 3), jnp.int32),
            pltpu.VMEM((PIECES, prows, width), jnp.bfloat16),
            pltpu.VMEM((PIECES, 2 * reach, prows, width), jnp.bfloat16),
            pltpu.VMEM((nsite, width, lanes), jnp.bfloat16),
            pltpu.VMEM((nblocks * vrows, lanes), jnp.float32),
            pltpu.VMEM((nsite - 1, vrows, lanes), jnp.bfloat16),
            pltpu.VMEM((PIECES, nsite - 1, 2 * reach * prows, lanes), jnp.bfloat16),
            pltpu.VMEM((nsite - 1, vrows, lanes), jnp.bfloat16),
            pltpu.VMEM((PIECES, nsite - 1, 2 * reach * prows, lanes), jnp.bfloat16),
            pltpu.SemaphoreType.DMA((2 + PIECES,)),
            pltpu.SemaphoreType.DMA((PIECES, 2 * reach)),
            pltpu.SemaphoreType.DMA((PIECES, 2 * reach)),
            pltpu.SemaphoreType.DMA((PIECES + 1, nsite - 1)),
            pltpu.SemaphoreType.DMA((PIECES + 1, nsite - 1)),
        ],
        compiler_params=pltpu.CompilerParams(
            collective_id=0, has_side_effects=True, vmem_limit_bytes=32 * 1024 * 1024
        ),
    )(
        pltpu.with_memory_space_constraint(jnp.transpose(w_modes, (0, 2, 3, 1)), pltpu.HBM),
        pltpu.with_memory_space_constraint(jnp.transpose(v_modes, (0, 2, 1, 3)), pltpu.HBM),
        pltpu.with_memory_space_constraint(momenta, pltpu.HBM),
    )
    return out.reshape(2, nph, rows, nblocks * vrows)


def solution(mesh):
    placed = (P(None, ("grp", "mode"), None, "site"), P(None, ("grp", "mode"), None, "site"), P())
    return jax.shard_map(
        functools.partial(shards, mesh.shape["mode"], mesh.shape["site"]),
        mesh=mesh,
        in_specs=placed,
        out_specs=P(None, None, ("grp", "mode", "site"), None),
        check_vma=False,
    )
```

```python
import functools

import jax
import jax.numpy as jnp
import numpy as np
from jax import lax
from jax.experimental import pallas as pl
from jax.experimental.pallas import tpu as pltpu
from jax.sharding import PartitionSpec as P

LAT = 96
REACH = 4
SPINS = 4
PIECES = 2
SIGNS = (-1.0, 1.0, 1.0, -1.0)
MESH = pl.DeviceIdType.MESH


def phase_table(mom_ref, nph, rows, sites):
    shape = (sites, nph * rows)
    index = lax.axis_index("site") * sites + lax.broadcasted_iota(jnp.int32, shape, 0)
    lane = lax.broadcasted_iota(jnp.int32, shape, 1)
    lat = jnp.full(shape, LAT, jnp.int32)
    xcoord = lax.rem(index, lat)
    upper = lax.div(index, lat)
    ycoord = lax.rem(upper, lat)
    zcoord = lax.div(upper, lat)
    total = jnp.zeros(shape, jnp.int32)
    for p in range(nph):
        here = mom_ref[p, 0] * xcoord + mom_ref[p, 1] * ycoord + mom_ref[p, 2] * zcoord
        total = jnp.where((lane >= p * rows) & (lane < (p + 1) * rows), here, total)
    wound = lax.rem(total, lat)
    wound = jnp.where(wound < 0, wound + LAT, wound)
    angle = (-2.0 * np.pi / LAT) * wound.astype(jnp.float32)
    return jnp.cos(angle), jnp.sin(angle)


def kernel(
    nmode, nsite, reach,
    w_hbm, v_hbm, mom_hbm, out_ref,
    w_ref, v_ref, mom_ref, packed, arrived, lhs, total,
    own_out, band_out, own_in, band_in,
    load_sem, vsend_sem, vrecv_sem, psend_sem, precv_sem,
):
    mode = lax.axis_index("mode")
    site = lax.axis_index("site")
    _, nsc, sites, wrows = w_ref.shape
    nph = mom_ref.shape[0]
    rows = wrows // nsite
    half = nph * rows
    npiece, prows, _ = packed.shape
    vrows = npiece * prows
    outgoing = [own_out] + [band_out.at[piece] for piece in range(npiece)]
    incoming = [own_in] + [band_in.at[piece] for piece in range(npiece)]
    step = 1 - 2 * lax.rem(site, 2) if nsite % 2 == 0 else 1

    def load_v(piece):
        return pltpu.make_async_copy(
            v_hbm.at[:, :, pl.ds(piece * prows, prows), :], v_ref.at[piece], load_sem.at[2 + piece]
        )

    for piece in range(npiece):
        load_v(piece).start()
    load_w = pltpu.make_async_copy(w_hbm, w_ref, load_sem.at[0])
    load_mom = pltpu.make_async_copy(mom_hbm, mom_ref, load_sem.at[1])
    load_mom.start()
    load_w.start()

    def mode_of(offset):
        return {"mode": lax.rem(mode + offset + nmode, nmode)}

    def site_of(distance):
        return lax.rem(site + step * distance + nsite, nsite)

    barrier = pltpu.get_barrier_semaphore()
    offsets = [o for o in range(-reach, reach + 1) if o != 0]
    for offset in offsets:
        pl.semaphore_signal(barrier, inc=1, device_id=mode_of(offset), device_id_type=MESH)
    for distance in range(1, nsite):
        pl.semaphore_signal(
            barrier, inc=1, device_id={"site": site_of(distance)}, device_id_type=MESH
        )

    def offset_at(index):
        return index - reach + jnp.where(index >= reach, 1, 0)

    def vcopy(piece, index):
        return pltpu.make_async_remote_copy(
            src_ref=packed.at[piece],
            dst_ref=arrived.at[piece, index],
            send_sem=vsend_sem.at[piece, index],
            recv_sem=vrecv_sem.at[piece, index],
            device_id=mode_of(-offset_at(index)),
            device_id_type=MESH,
        )

    if reach == 1 and npiece == 2:
        last = mode == nmode - 1
        end = (mode == 0) | last
        around = jnp.where(last, 0, 1)
        stages = [
            [(0, jnp.where(end, around, 0)), (jnp.where(end, 1, 0), jnp.where(end, around, 1))],
            [(jnp.where(end, 0, 1), jnp.where(end, 1 - around, 0)), (1, jnp.where(end, 1 - around, 1))],
        ]
    else:
        stages = [[(piece, index) for index in range(len(offsets))] for piece in range(npiece)]

    for piece in range(npiece):
        load_v(piece).wait()
        for sc in range(nsc):
            packed[piece, :, sc * 2 * sites : (sc + 1) * 2 * sites] = jnp.concatenate(
                [v_ref[piece, 0, sc], v_ref[piece, 1, sc]], axis=1
            )
    pl.semaphore_wait(barrier, len(offsets) + nsite - 1)
    for piece, index in stages[0]:
        vcopy(piece, index).start()

    load_mom.wait()
    cosine, sine = phase_table(mom_ref, nph, rows, sites)
    shape = (wrows, nsite * half)
    mode_row = lax.broadcasted_iota(jnp.int32, shape, 0)
    lane = lax.broadcasted_iota(jnp.int32, shape, 1)
    spread = jnp.zeros(shape, jnp.float32)
    for piece in range(nsite * nph):
        source = lane - piece * rows + (piece // nph) * rows
        inside = (lane >= piece * rows) & (lane < (piece + 1) * rows)
        spread = jnp.where(inside & (mode_row == source), 1.0, spread)
    spread = spread.astype(jnp.bfloat16)

    load_w.wait()
    colours = nsc // SPINS
    for spin in range(SPINS):
        taken = slice(colours * (SPINS - 1 - spin), colours * (SPINS - spin))
        both = jnp.concatenate(
            [w_ref[part, taken].reshape(colours * sites, wrows) for part in range(2)], axis=0
        )
        wide = jnp.dot(both, spread, preferred_element_type=jnp.float32)
        scos, ssin = SIGNS[spin] * cosine, SIGNS[spin] * sine
        for colour in range(colours):
            wreal = wide[colour * sites : (colour + 1) * sites]
            wimag = wide[(colours + colour) * sites : (colours + colour + 1) * sites]
            base = (colours * spin + colour) * 2 * sites
            top, low = pl.ds(base, sites), pl.ds(base + sites, sites)
            for s in range(nsite):
                part = slice(s * half, (s + 1) * half)
                areal = wreal[:, part] * scos + wimag[:, part] * ssin
                aimag = wreal[:, part] * ssin - wimag[:, part] * scos
                lhs[s, top, 0:half] = areal.astype(jnp.bfloat16)
                lhs[s, top, half : 2 * half] = aimag.astype(jnp.bfloat16)
                lhs[s, low, 0:half] = (-aimag).astype(jnp.bfloat16)
                lhs[s, low, half : 2 * half] = areal.astype(jnp.bfloat16)

    distances = list(range(nsite - 1, 0, -1))
    if nsite > 2:
        distances.remove(nsite // 2)
        distances.insert(0, nsite // 2)

    def partial_copy(group, distance):
        return pltpu.make_async_remote_copy(
            src_ref=outgoing[group].at[distance - 1],
            dst_ref=incoming[group].at[distance - 1],
            send_sem=psend_sem.at[group, distance - 1],
            recv_sem=precv_sem.at[group, distance - 1],
            device_id={"site": site_of(distance)},
            device_id_type=MESH,
        )

    def handle(group, block):
        for distance in distances:
            outgoing[group][distance - 1] = jnp.dot(
                block, lhs[site_of(distance)], preferred_element_type=jnp.float32
            ).astype(jnp.bfloat16)
            partial_copy(group, distance).start()
        own = jnp.dot(block, lhs[site], preferred_element_type=jnp.float32)
        for start, stop, column in places(group):
            total[column : column + stop - start, :] = own[start:stop]

    def places(group):
        if group == 0:
            return [(0, vrows, reach * vrows)]
        return [
            (i * prows, (i + 1) * prows, (o + reach) * vrows + (group - 1) * prows)
            for i, o in enumerate(offsets)
        ]

    def gather(group):
        for distance in distances:
            partial_copy(group, distance).wait_recv()
        for start, stop, column in places(group):
            value = total[column : column + stop - start, :]
            for distance in distances:
                value = value + incoming[group][distance - 1, start:stop].astype(jnp.float32)
            total[column : column + stop - start, :] = value

    def next_stage(stage):
        for piece, index in stages[stage - 1]:
            vcopy(piece, index).wait_send()
        for piece, index in stages[stage]:
            vcopy(piece, index).start()

    next_stage(1)
    handle(0, packed[...].reshape(vrows, -1))
    for piece in range(npiece):
        if 1 <= piece < npiece - 1:
            next_stage(piece + 1)
        for index in range(len(offsets)):
            vcopy(piece, index).wait_recv()
        handle(piece + 1, arrived[piece].reshape(len(offsets) * prows, -1))
        gather(piece)
    gather(npiece)
    out_ref[...] = total[...].T
    for piece, index in stages[-1]:
        vcopy(piece, index).wait_send()
    for group in range(npiece + 1):
        for distance in distances:
            partial_copy(group, distance).wait_send()


def shards(nmode, nsite, w_modes, v_modes, momenta):
    _, wrows, nsc, sites = w_modes.shape
    vrows = v_modes.shape[1]
    nph = momenta.shape[0]
    reach = min(REACH, (nmode - 1) // 2)
    nblocks = 2 * reach + 1
    rows = wrows // nsite
    width = 2 * nsc * sites
    lanes = 2 * nph * rows
    prows = vrows // PIECES
    out = pl.pallas_call(
        functools.partial(kernel, nmode, nsite, reach),
        out_shape=jax.ShapeDtypeStruct((lanes, nblocks * vrows), jnp.float32),
        in_specs=[
            pl.BlockSpec(memory_space=pltpu.HBM),
            pl.BlockSpec(memory_space=pltpu.HBM),
            pl.BlockSpec(memory_space=pltpu.HBM),
        ],
        out_specs=pl.BlockSpec(memory_space=pltpu.VMEM),
        scratch_shapes=[
            pltpu.VMEM((2, nsc, sites, wrows), jnp.bfloat16),
            pltpu.VMEM((PIECES, 2, nsc, prows, sites), jnp.bfloat16),
            pltpu.SMEM((nph, 3), jnp.int32),
            pltpu.VMEM((PIECES, prows, width), jnp.bfloat16),
            pltpu.VMEM((PIECES, 2 * reach, prows, width), jnp.bfloat16),
            pltpu.VMEM((nsite, width, lanes), jnp.bfloat16),
            pltpu.VMEM((nblocks * vrows, lanes), jnp.float32),
            pltpu.VMEM((nsite - 1, vrows, lanes), jnp.bfloat16),
            pltpu.VMEM((PIECES, nsite - 1, 2 * reach * prows, lanes), jnp.bfloat16),
            pltpu.VMEM((nsite - 1, vrows, lanes), jnp.bfloat16),
            pltpu.VMEM((PIECES, nsite - 1, 2 * reach * prows, lanes), jnp.bfloat16),
            pltpu.SemaphoreType.DMA((2 + PIECES,)),
            pltpu.SemaphoreType.DMA((PIECES, 2 * reach)),
            pltpu.SemaphoreType.DMA((PIECES, 2 * reach)),
            pltpu.SemaphoreType.DMA((PIECES + 1, nsite - 1)),
            pltpu.SemaphoreType.DMA((PIECES + 1, nsite - 1)),
        ],
        compiler_params=pltpu.CompilerParams(
            collective_id=0, has_side_effects=True, vmem_limit_bytes=32 * 1024 * 1024
        ),
    )(
        pltpu.with_memory_space_constraint(jnp.transpose(w_modes, (0, 2, 3, 1)), pltpu.HBM),
        pltpu.with_memory_space_constraint(jnp.transpose(v_modes, (0, 2, 1, 3)), pltpu.HBM),
        pltpu.with_memory_space_constraint(momenta, pltpu.HBM),
    )
    return out.reshape(2, nph, rows, nblocks * vrows)


def solution(mesh):
    placed = (P(None, ("grp", "mode"), None, "site"), P(None, ("grp", "mode"), None, "site"), P())
    return jax.shard_map(
        functools.partial(shards, mesh.shape["mode"], mesh.shape["site"]),
        mesh=mesh,
        in_specs=placed,
        out_specs=P(None, None, ("grp", "mode", "site"), None),
        check_vma=False,
    )
```

```python
import functools

import jax
import jax.numpy as jnp
import numpy as np
from jax import lax
from jax.experimental import pallas as pl
from jax.experimental.pallas import tpu as pltpu
from jax.sharding import PartitionSpec as P

LAT = 96
REACH = 4
SPINS = 4
CUTS = (2, 4, 4)
SIGNS = (-1.0, 1.0, 1.0, -1.0)
MESH = pl.DeviceIdType.MESH


def spans_of(vrows):
    spans = []
    first = 0
    for cut in CUTS:
        spans.append((first, vrows // cut))
        first += vrows // cut
    return spans


def phase_table(mom_ref, nph, rows, sites):
    shape = (sites, nph * rows)
    index = lax.axis_index("site") * sites + lax.broadcasted_iota(jnp.int32, shape, 0)
    lane = lax.broadcasted_iota(jnp.int32, shape, 1)
    lat = jnp.full(shape, LAT, jnp.int32)
    xcoord = lax.rem(index, lat)
    upper = lax.div(index, lat)
    ycoord = lax.rem(upper, lat)
    zcoord = lax.div(upper, lat)
    total = jnp.zeros(shape, jnp.int32)
    for p in range(nph):
        here = mom_ref[p, 0] * xcoord + mom_ref[p, 1] * ycoord + mom_ref[p, 2] * zcoord
        total = jnp.where((lane >= p * rows) & (lane < (p + 1) * rows), here, total)
    wound = lax.rem(total, lat)
    wound = jnp.where(wound < 0, wound + LAT, wound)
    angle = (-2.0 * np.pi / LAT) * wound.astype(jnp.float32)
    return jnp.cos(angle), jnp.sin(angle)


def kernel(
    nmode, nsite, reach,
    w_hbm, v_hbm, mom_hbm, out_ref,
    w_ref, v_ref, mom_ref, packed, arrived, lhs, total,
    own_out, band_out, own_in, band_in,
    load_sem, vsend_sem, vrecv_sem, psend_sem, precv_sem,
):
    mode = lax.axis_index("mode")
    site = lax.axis_index("site")
    _, nsc, sites, wrows = w_ref.shape
    nph = mom_ref.shape[0]
    rows = wrows // nsite
    half = nph * rows
    vrows = packed.shape[0]
    spans = spans_of(vrows)
    npiece = len(spans)
    wide_spans = [pl.ds(2 * reach * first, 2 * reach * count) for first, count in spans]
    outgoing = [own_out] + [band_out.at[:, wide] for wide in wide_spans]
    incoming = [own_in] + [band_in.at[:, wide] for wide in wide_spans]
    step = 1 - 2 * lax.rem(site, 2) if nsite % 2 == 0 else 1

    def load_v(piece):
        taken = pl.ds(*spans[piece])
        return pltpu.make_async_copy(
            v_hbm.at[:, :, taken, :], v_ref.at[:, :, taken, :], load_sem.at[2 + piece]
        )

    for piece in range(npiece):
        load_v(piece).start()
    load_w = pltpu.make_async_copy(w_hbm, w_ref, load_sem.at[0])
    load_mom = pltpu.make_async_copy(mom_hbm, mom_ref, load_sem.at[1])
    load_mom.start()
    load_w.start()

    def mode_of(offset):
        return {"mode": lax.rem(mode + offset + nmode, nmode)}

    def site_of(distance):
        return lax.rem(site + step * distance + nsite, nsite)

    barrier = pltpu.get_barrier_semaphore()
    offsets = [o for o in range(-reach, reach + 1) if o != 0]
    for offset in offsets:
        pl.semaphore_signal(barrier, inc=1, device_id=mode_of(offset), device_id_type=MESH)
    for distance in range(1, nsite):
        pl.semaphore_signal(
            barrier, inc=1, device_id={"site": site_of(distance)}, device_id_type=MESH
        )

    def vcopy(piece, index):
        first, count = spans[piece]
        return pltpu.make_async_remote_copy(
            src_ref=packed.at[pl.ds(first, count)],
            dst_ref=arrived.at[pl.ds(2 * reach * first + index * count, count)],
            send_sem=vsend_sem.at[piece, index],
            recv_sem=vrecv_sem.at[piece, index],
            device_id=mode_of(-offsets[index]),
            device_id_type=MESH,
        )

    for piece in range(npiece):
        load_v(piece).wait()
        first, count = spans[piece]
        for sc in range(nsc):
            packed[first : first + count, sc * 2 * sites : (sc + 1) * 2 * sites] = jnp.concatenate(
                [v_ref[part, sc, first : first + count] for part in range(2)], axis=1
            )
        if piece == 0:
            pl.semaphore_wait(barrier, len(offsets) + nsite - 1)
            for index in range(len(offsets)):
                vcopy(piece, index).start()

    load_mom.wait()
    cosine, sine = phase_table(mom_ref, nph, rows, sites)
    shape = (wrows, nsite * half)
    mode_row = lax.broadcasted_iota(jnp.int32, shape, 0)
    lane = lax.broadcasted_iota(jnp.int32, shape, 1)
    spread = jnp.zeros(shape, jnp.float32)
    for piece in range(nsite * nph):
        source = lane - piece * rows + (piece // nph) * rows
        inside = (lane >= piece * rows) & (lane < (piece + 1) * rows)
        spread = jnp.where(inside & (mode_row == source), 1.0, spread)
    spread = spread.astype(jnp.bfloat16)

    load_w.wait()
    colours = nsc // SPINS
    for spin in range(SPINS):
        taken = slice(colours * (SPINS - 1 - spin), colours * (SPINS - spin))
        both = jnp.concatenate(
            [w_ref[part, taken].reshape(colours * sites, wrows) for part in range(2)], axis=0
        )
        wide = jnp.dot(both, spread, preferred_element_type=jnp.float32)
        scos, ssin = SIGNS[spin] * cosine, SIGNS[spin] * sine
        for colour in range(colours):
            wreal = wide[colour * sites : (colour + 1) * sites]
            wimag = wide[(colours + colour) * sites : (colours + colour + 1) * sites]
            base = (colours * spin + colour) * 2 * sites
            top, low = pl.ds(base, sites), pl.ds(base + sites, sites)
            for s in range(nsite):
                part = slice(s * half, (s + 1) * half)
                areal = wreal[:, part] * scos + wimag[:, part] * ssin
                aimag = wreal[:, part] * ssin - wimag[:, part] * scos
                lhs[s, top, 0:half] = areal.astype(jnp.bfloat16)
                lhs[s, top, half : 2 * half] = aimag.astype(jnp.bfloat16)
                lhs[s, low, 0:half] = (-aimag).astype(jnp.bfloat16)
                lhs[s, low, half : 2 * half] = areal.astype(jnp.bfloat16)

    distances = list(range(nsite - 1, 0, -1))
    if nsite > 2:
        distances.remove(nsite // 2)
        distances.insert(0, nsite // 2)

    def partial_copy(group, distance):
        return pltpu.make_async_remote_copy(
            src_ref=outgoing[group].at[distance - 1],
            dst_ref=incoming[group].at[distance - 1],
            send_sem=psend_sem.at[group, distance - 1],
            recv_sem=precv_sem.at[group, distance - 1],
            device_id={"site": site_of(distance)},
            device_id_type=MESH,
        )

    def handle(group, block):
        for distance in distances:
            outgoing[group][distance - 1] = jnp.dot(
                block, lhs[site_of(distance)], preferred_element_type=jnp.float32
            ).astype(jnp.bfloat16)
            partial_copy(group, distance).start()
        own = jnp.dot(block, lhs[site], preferred_element_type=jnp.float32)
        for start, stop, column in places(group):
            total[column : column + stop - start, :] = own[start:stop]

    def places(group):
        if group == 0:
            return [(0, vrows, reach * vrows)]
        first, count = spans[group - 1]
        return [
            (i * count, (i + 1) * count, (o + reach) * vrows + first)
            for i, o in enumerate(offsets)
        ]

    def gather(group):
        for distance in distances:
            partial_copy(group, distance).wait_recv()
        for start, stop, column in places(group):
            value = total[column : column + stop - start, :]
            for distance in distances:
                value = value + incoming[group][distance - 1, start:stop].astype(jnp.float32)
            total[column : column + stop - start, :] = value

    def next_piece(piece):
        for index in range(len(offsets)):
            vcopy(piece - 1, index).wait_send()
            vcopy(piece, index).start()

    next_piece(1)
    handle(0, packed[...])
    for piece in range(npiece):
        for index in range(len(offsets)):
            vcopy(piece, index).wait_recv()
        handle(piece + 1, arrived[wide_spans[piece], :])
        if 1 <= piece + 1 < npiece - 1:
            next_piece(piece + 2)
        gather(piece)
    gather(npiece)
    out_ref[...] = total[...].T
    for index in range(len(offsets)):
        vcopy(npiece - 1, index).wait_send()
    for group in range(npiece + 1):
        for distance in distances:
            partial_copy(group, distance).wait_send()


def shards(nmode, nsite, w_modes, v_modes, momenta):
    _, wrows, nsc, sites = w_modes.shape
    vrows = v_modes.shape[1]
    nph = momenta.shape[0]
    reach = min(REACH, (nmode - 1) // 2)
    nblocks = 2 * reach + 1
    rows = wrows // nsite
    width = 2 * nsc * sites
    lanes = 2 * nph * rows
    pieces = len(CUTS)
    out = pl.pallas_call(
        functools.partial(kernel, nmode, nsite, reach),
        out_shape=jax.ShapeDtypeStruct((lanes, nblocks * vrows), jnp.float32),
        in_specs=[
            pl.BlockSpec(memory_space=pltpu.HBM),
            pl.BlockSpec(memory_space=pltpu.HBM),
            pl.BlockSpec(memory_space=pltpu.HBM),
        ],
        out_specs=pl.BlockSpec(memory_space=pltpu.VMEM),
        scratch_shapes=[
            pltpu.VMEM((2, nsc, sites, wrows), jnp.bfloat16),
            pltpu.VMEM((2, nsc, vrows, sites), jnp.bfloat16),
            pltpu.SMEM((nph, 3), jnp.int32),
            pltpu.VMEM((vrows, width), jnp.bfloat16),
            pltpu.VMEM((2 * reach * vrows, width), jnp.bfloat16),
            pltpu.VMEM((nsite, width, lanes), jnp.bfloat16),
            pltpu.VMEM((nblocks * vrows, lanes), jnp.float32),
            pltpu.VMEM((nsite - 1, vrows, lanes), jnp.bfloat16),
            pltpu.VMEM((nsite - 1, 2 * reach * vrows, lanes), jnp.bfloat16),
            pltpu.VMEM((nsite - 1, vrows, lanes), jnp.bfloat16),
            pltpu.VMEM((nsite - 1, 2 * reach * vrows, lanes), jnp.bfloat16),
            pltpu.SemaphoreType.DMA((2 + pieces,)),
            pltpu.SemaphoreType.DMA((pieces, 2 * reach)),
            pltpu.SemaphoreType.DMA((pieces, 2 * reach)),
            pltpu.SemaphoreType.DMA((pieces + 1, nsite - 1)),
            pltpu.SemaphoreType.DMA((pieces + 1, nsite - 1)),
        ],
        compiler_params=pltpu.CompilerParams(
            collective_id=0, has_side_effects=True, vmem_limit_bytes=32 * 1024 * 1024
        ),
    )(
        pltpu.with_memory_space_constraint(jnp.transpose(w_modes, (0, 2, 3, 1)), pltpu.HBM),
        pltpu.with_memory_space_constraint(jnp.transpose(v_modes, (0, 2, 1, 3)), pltpu.HBM),
        pltpu.with_memory_space_constraint(momenta, pltpu.HBM),
    )
    return out.reshape(2, nph, rows, nblocks * vrows)


def solution(mesh):
    placed = (P(None, ("grp", "mode"), None, "site"), P(None, ("grp", "mode"), None, "site"), P())
    return jax.shard_map(
        functools.partial(shards, mesh.shape["mode"], mesh.shape["site"]),
        mesh=mesh,
        in_specs=placed,
        out_specs=P(None, None, ("grp", "mode", "site"), None),
        check_vma=False,
    )
```

```python
import functools

import jax
import jax.numpy as jnp
import numpy as np
from jax import lax
from jax.experimental import pallas as pl
from jax.experimental.pallas import tpu as pltpu
from jax.sharding import PartitionSpec as P

LAT = 96
REACH = 4
SPINS = 4
CUTS = (2, 2)
SIGNS = (-1.0, 1.0, 1.0, -1.0)
MESH = pl.DeviceIdType.MESH


def spans_of(vrows):
    spans = []
    first = 0
    for cut in CUTS:
        spans.append((first, vrows // cut))
        first += vrows // cut
    return spans


def phase_table(mom_ref, nph, rows, sites):
    shape = (sites, nph * rows)
    index = lax.axis_index("site") * sites + lax.broadcasted_iota(jnp.int32, shape, 0)
    lane = lax.broadcasted_iota(jnp.int32, shape, 1)
    lat = jnp.full(shape, LAT, jnp.int32)
    xcoord = lax.rem(index, lat)
    upper = lax.div(index, lat)
    ycoord = lax.rem(upper, lat)
    zcoord = lax.div(upper, lat)
    total = jnp.zeros(shape, jnp.int32)
    for p in range(nph):
        here = mom_ref[p, 0] * xcoord + mom_ref[p, 1] * ycoord + mom_ref[p, 2] * zcoord
        total = jnp.where((lane >= p * rows) & (lane < (p + 1) * rows), here, total)
    wound = lax.rem(total, lat)
    wound = jnp.where(wound < 0, wound + LAT, wound)
    angle = (-2.0 * np.pi / LAT) * wound.astype(jnp.float32)
    return jnp.cos(angle), jnp.sin(angle)


def kernel(
    nmode, nsite, reach,
    w_hbm, v_hbm, mom_hbm, out_ref,
    w_ref, v_ref, mom_ref, packed, arrived, lhs, total,
    own_out, band_out, own_in, band_in,
    load_sem, vsend_sem, vrecv_sem, psend_sem, precv_sem,
):
    mode = lax.axis_index("mode")
    site = lax.axis_index("site")
    _, nsc, sites, wrows = w_ref.shape
    nph = mom_ref.shape[0]
    rows = wrows // nsite
    half = nph * rows
    vrows = packed.shape[0]
    spans = spans_of(vrows)
    npiece = len(spans)
    wide_spans = [pl.ds(2 * reach * first, 2 * reach * count) for first, count in spans]
    outgoing = [own_out] + [band_out.at[:, wide] for wide in wide_spans]
    incoming = [own_in] + [band_in.at[:, wide] for wide in wide_spans]
    step = 1 - 2 * lax.rem(site, 2) if nsite % 2 == 0 else 1

    def load_v(piece):
        taken = pl.ds(*spans[piece])
        return pltpu.make_async_copy(
            v_hbm.at[:, :, taken, :], v_ref.at[:, :, taken, :], load_sem.at[2 + piece]
        )

    for piece in range(npiece):
        load_v(piece).start()
    load_w = pltpu.make_async_copy(w_hbm, w_ref, load_sem.at[0])
    load_mom = pltpu.make_async_copy(mom_hbm, mom_ref, load_sem.at[1])
    load_mom.start()
    load_w.start()

    def mode_of(offset):
        return {"mode": lax.rem(mode + offset + nmode, nmode)}

    def site_of(distance):
        return lax.rem(site + step * distance + nsite, nsite)

    barrier = pltpu.get_barrier_semaphore()
    offsets = [o for o in range(-reach, reach + 1) if o != 0]
    for offset in offsets:
        pl.semaphore_signal(barrier, inc=1, device_id=mode_of(offset), device_id_type=MESH)
    for distance in range(1, nsite):
        pl.semaphore_signal(
            barrier, inc=1, device_id={"site": site_of(distance)}, device_id_type=MESH
        )

    def vcopy(piece, index):
        first, count = spans[piece]
        return pltpu.make_async_remote_copy(
            src_ref=packed.at[pl.ds(first, count)],
            dst_ref=arrived.at[pl.ds(2 * reach * first + index * count, count)],
            send_sem=vsend_sem.at[piece, index],
            recv_sem=vrecv_sem.at[piece, index],
            device_id=mode_of(-offsets[index]),
            device_id_type=MESH,
        )

    for piece in range(npiece):
        load_v(piece).wait()
        first, count = spans[piece]
        for sc in range(nsc):
            packed[first : first + count, sc * 2 * sites : (sc + 1) * 2 * sites] = jnp.concatenate(
                [v_ref[part, sc, first : first + count] for part in range(2)], axis=1
            )
        if piece == 0:
            pl.semaphore_wait(barrier, len(offsets) + nsite - 1)
        for index in range(len(offsets)):
            vcopy(piece, index).start()

    load_mom.wait()
    cosine, sine = phase_table(mom_ref, nph, rows, sites)
    shape = (wrows, nsite * half)
    mode_row = lax.broadcasted_iota(jnp.int32, shape, 0)
    lane = lax.broadcasted_iota(jnp.int32, shape, 1)
    spread = jnp.zeros(shape, jnp.float32)
    for piece in range(nsite * nph):
        source = lane - piece * rows + (piece // nph) * rows
        inside = (lane >= piece * rows) & (lane < (piece + 1) * rows)
        spread = jnp.where(inside & (mode_row == source), 1.0, spread)
    spread = spread.astype(jnp.bfloat16)

    load_w.wait()
    colours = nsc // SPINS
    for spin in range(SPINS):
        taken = slice(colours * (SPINS - 1 - spin), colours * (SPINS - spin))
        both = jnp.concatenate(
            [w_ref[part, taken].reshape(colours * sites, wrows) for part in range(2)], axis=0
        )
        wide = jnp.dot(both, spread, preferred_element_type=jnp.float32)
        scos, ssin = SIGNS[spin] * cosine, SIGNS[spin] * sine
        for colour in range(colours):
            wreal = wide[colour * sites : (colour + 1) * sites]
            wimag = wide[(colours + colour) * sites : (colours + colour + 1) * sites]
            base = (colours * spin + colour) * 2 * sites
            top, low = pl.ds(base, sites), pl.ds(base + sites, sites)
            for s in range(nsite):
                part = slice(s * half, (s + 1) * half)
                areal = wreal[:, part] * scos + wimag[:, part] * ssin
                aimag = wreal[:, part] * ssin - wimag[:, part] * scos
                lhs[s, top, 0:half] = areal.astype(jnp.bfloat16)
                lhs[s, top, half : 2 * half] = aimag.astype(jnp.bfloat16)
                lhs[s, low, 0:half] = (-aimag).astype(jnp.bfloat16)
                lhs[s, low, half : 2 * half] = areal.astype(jnp.bfloat16)

    distances = list(range(nsite - 1, 0, -1))
    if nsite > 2:
        distances.remove(nsite // 2)
        distances.insert(0, nsite // 2)

    def partial_copy(group, distance):
        return pltpu.make_async_remote_copy(
            src_ref=outgoing[group].at[distance - 1],
            dst_ref=incoming[group].at[distance - 1],
            send_sem=psend_sem.at[group, distance - 1],
            recv_sem=precv_sem.at[group, distance - 1],
            device_id={"site": site_of(distance)},
            device_id_type=MESH,
        )

    def handle(group, block):
        for distance in distances:
            outgoing[group][distance - 1] = jnp.dot(
                block, lhs[site_of(distance)], preferred_element_type=jnp.float32
            ).astype(jnp.bfloat16)
            partial_copy(group, distance).start()
        own = jnp.dot(block, lhs[site], preferred_element_type=jnp.float32)
        for start, stop, column in places(group):
            total[column : column + stop - start, :] = own[start:stop]

    def places(group):
        if group == 0:
            return [(0, vrows, reach * vrows)]
        first, count = spans[group - 1]
        return [
            (i * count, (i + 1) * count, (o + reach) * vrows + first)
            for i, o in enumerate(offsets)
        ]

    def gather(group):
        for distance in distances:
            partial_copy(group, distance).wait_recv()
        for start, stop, column in places(group):
            value = total[column : column + stop - start, :]
            for distance in distances:
                value = value + incoming[group][distance - 1, start:stop].astype(jnp.float32)
            total[column : column + stop - start, :] = value

    handle(0, packed[...])
    for piece in range(npiece):
        for index in range(len(offsets)):
            vcopy(piece, index).wait_recv()
        handle(piece + 1, arrived[wide_spans[piece], :])
        gather(piece)
    gather(npiece)
    out_ref[...] = total[...].T
    for piece in range(npiece):
        for index in range(len(offsets)):
            vcopy(piece, index).wait_send()
    for group in range(npiece + 1):
        for distance in distances:
            partial_copy(group, distance).wait_send()


def shards(nmode, nsite, w_modes, v_modes, momenta):
    _, wrows, nsc, sites = w_modes.shape
    vrows = v_modes.shape[1]
    nph = momenta.shape[0]
    reach = min(REACH, (nmode - 1) // 2)
    nblocks = 2 * reach + 1
    rows = wrows // nsite
    width = 2 * nsc * sites
    lanes = 2 * nph * rows
    pieces = len(CUTS)
    out = pl.pallas_call(
        functools.partial(kernel, nmode, nsite, reach),
        out_shape=jax.ShapeDtypeStruct((lanes, nblocks * vrows), jnp.float32),
        in_specs=[
            pl.BlockSpec(memory_space=pltpu.HBM),
            pl.BlockSpec(memory_space=pltpu.HBM),
            pl.BlockSpec(memory_space=pltpu.HBM),
        ],
        out_specs=pl.BlockSpec(memory_space=pltpu.VMEM),
        scratch_shapes=[
            pltpu.VMEM((2, nsc, sites, wrows), jnp.bfloat16),
            pltpu.VMEM((2, nsc, vrows, sites), jnp.bfloat16),
            pltpu.SMEM((nph, 3), jnp.int32),
            pltpu.VMEM((vrows, width), jnp.bfloat16),
            pltpu.VMEM((2 * reach * vrows, width), jnp.bfloat16),
            pltpu.VMEM((nsite, width, lanes), jnp.bfloat16),
            pltpu.VMEM((nblocks * vrows, lanes), jnp.float32),
            pltpu.VMEM((nsite - 1, vrows, lanes), jnp.bfloat16),
            pltpu.VMEM((nsite - 1, 2 * reach * vrows, lanes), jnp.bfloat16),
            pltpu.VMEM((nsite - 1, vrows, lanes), jnp.bfloat16),
            pltpu.VMEM((nsite - 1, 2 * reach * vrows, lanes), jnp.bfloat16),
            pltpu.SemaphoreType.DMA((2 + pieces,)),
            pltpu.SemaphoreType.DMA((pieces, 2 * reach)),
            pltpu.SemaphoreType.DMA((pieces, 2 * reach)),
            pltpu.SemaphoreType.DMA((pieces + 1, nsite - 1)),
            pltpu.SemaphoreType.DMA((pieces + 1, nsite - 1)),
        ],
        compiler_params=pltpu.CompilerParams(
            collective_id=0, has_side_effects=True, vmem_limit_bytes=32 * 1024 * 1024
        ),
    )(
        pltpu.with_memory_space_constraint(jnp.transpose(w_modes, (0, 2, 3, 1)), pltpu.HBM),
        pltpu.with_memory_space_constraint(jnp.transpose(v_modes, (0, 2, 1, 3)), pltpu.HBM),
        pltpu.with_memory_space_constraint(momenta, pltpu.HBM),
    )
    return out.reshape(2, nph, rows, nblocks * vrows)


def solution(mesh):
    placed = (P(None, ("grp", "mode"), None, "site"), P(None, ("grp", "mode"), None, "site"), P())
    return jax.shard_map(
        functools.partial(shards, mesh.shape["mode"], mesh.shape["site"]),
        mesh=mesh,
        in_specs=placed,
        out_specs=P(None, None, ("grp", "mode", "site"), None),
        check_vma=False,
    )
```

```python
import functools

import jax
import jax.numpy as jnp
import numpy as np
from jax import lax
from jax.experimental import pallas as pl
from jax.experimental.pallas import tpu as pltpu
from jax.sharding import PartitionSpec as P

LAT = 96
REACH = 4
SPINS = 4
QUARTERS = (3, 1)
SIGNS = (-1.0, 1.0, 1.0, -1.0)
MESH = pl.DeviceIdType.MESH


def spans_of(vrows):
    spans = []
    first = 0
    for quarters in QUARTERS:
        spans.append((first, vrows * quarters // 4))
        first += vrows * quarters // 4
    return spans


def phase_table(mom_ref, nph, rows, sites):
    shape = (sites, nph * rows)
    index = lax.axis_index("site") * sites + lax.broadcasted_iota(jnp.int32, shape, 0)
    lane = lax.broadcasted_iota(jnp.int32, shape, 1)
    lat = jnp.full(shape, LAT, jnp.int32)
    xcoord = lax.rem(index, lat)
    upper = lax.div(index, lat)
    ycoord = lax.rem(upper, lat)
    zcoord = lax.div(upper, lat)
    total = jnp.zeros(shape, jnp.int32)
    for p in range(nph):
        here = mom_ref[p, 0] * xcoord + mom_ref[p, 1] * ycoord + mom_ref[p, 2] * zcoord
        total = jnp.where((lane >= p * rows) & (lane < (p + 1) * rows), here, total)
    wound = lax.rem(total, lat)
    wound = jnp.where(wound < 0, wound + LAT, wound)
    angle = (-2.0 * np.pi / LAT) * wound.astype(jnp.float32)
    return jnp.cos(angle), jnp.sin(angle)


def kernel(
    nmode, nsite, reach,
    w_hbm, v_hbm, mom_hbm, out_ref,
    w_ref, v_ref, mom_ref, packed, arrived, lhs, total,
    own_out, band_out, own_in, band_in,
    load_sem, vsend_sem, vrecv_sem, psend_sem, precv_sem,
):
    mode = lax.axis_index("mode")
    site = lax.axis_index("site")
    _, nsc, sites, wrows = w_ref.shape
    nph = mom_ref.shape[0]
    rows = wrows // nsite
    half = nph * rows
    vrows = packed.shape[0]
    spans = spans_of(vrows)
    npiece = len(spans)
    wide_spans = [pl.ds(2 * reach * first, 2 * reach * count) for first, count in spans]
    outgoing = [own_out] + [band_out.at[:, wide] for wide in wide_spans]
    incoming = [own_in] + [band_in.at[:, wide] for wide in wide_spans]
    step = 1 - 2 * lax.rem(site, 2) if nsite % 2 == 0 else 1

    def load_v(piece):
        taken = pl.ds(*spans[piece])
        return pltpu.make_async_copy(
            v_hbm.at[:, :, taken, :], v_ref.at[:, :, taken, :], load_sem.at[2 + piece]
        )

    for piece in range(npiece):
        load_v(piece).start()
    load_w = pltpu.make_async_copy(w_hbm, w_ref, load_sem.at[0])
    load_mom = pltpu.make_async_copy(mom_hbm, mom_ref, load_sem.at[1])
    load_mom.start()
    load_w.start()

    def mode_of(offset):
        return {"mode": lax.rem(mode + offset + nmode, nmode)}

    def site_of(distance):
        return lax.rem(site + step * distance + nsite, nsite)

    barrier = pltpu.get_barrier_semaphore()
    offsets = [o for o in range(-reach, reach + 1) if o != 0]
    for offset in offsets:
        pl.semaphore_signal(barrier, inc=1, device_id=mode_of(offset), device_id_type=MESH)
    for distance in range(1, nsite):
        pl.semaphore_signal(
            barrier, inc=1, device_id={"site": site_of(distance)}, device_id_type=MESH
        )

    def vcopy(piece, index):
        first, count = spans[piece]
        return pltpu.make_async_remote_copy(
            src_ref=packed.at[pl.ds(first, count)],
            dst_ref=arrived.at[pl.ds(2 * reach * first + index * count, count)],
            send_sem=vsend_sem.at[piece, index],
            recv_sem=vrecv_sem.at[piece, index],
            device_id=mode_of(-offsets[index]),
            device_id_type=MESH,
        )

    for piece in range(npiece):
        load_v(piece).wait()
        first, count = spans[piece]
        for sc in range(nsc):
            packed[first : first + count, sc * 2 * sites : (sc + 1) * 2 * sites] = jnp.concatenate(
                [v_ref[part, sc, first : first + count] for part in range(2)], axis=1
            )
        if piece == 0:
            pl.semaphore_wait(barrier, len(offsets) + nsite - 1)
        for index in range(len(offsets)):
            vcopy(piece, index).start()

    load_mom.wait()
    cosine, sine = phase_table(mom_ref, nph, rows, sites)
    shape = (wrows, nsite * half)
    mode_row = lax.broadcasted_iota(jnp.int32, shape, 0)
    lane = lax.broadcasted_iota(jnp.int32, shape, 1)
    spread = jnp.zeros(shape, jnp.float32)
    for piece in range(nsite * nph):
        source = lane - piece * rows + (piece // nph) * rows
        inside = (lane >= piece * rows) & (lane < (piece + 1) * rows)
        spread = jnp.where(inside & (mode_row == source), 1.0, spread)
    spread = spread.astype(jnp.bfloat16)

    load_w.wait()
    colours = nsc // SPINS
    for spin in range(SPINS):
        taken = slice(colours * (SPINS - 1 - spin), colours * (SPINS - spin))
        both = jnp.concatenate(
            [w_ref[part, taken].reshape(colours * sites, wrows) for part in range(2)], axis=0
        )
        wide = jnp.dot(both, spread, preferred_element_type=jnp.float32)
        scos, ssin = SIGNS[spin] * cosine, SIGNS[spin] * sine
        for colour in range(colours):
            wreal = wide[colour * sites : (colour + 1) * sites]
            wimag = wide[(colours + colour) * sites : (colours + colour + 1) * sites]
            base = (colours * spin + colour) * 2 * sites
            top, low = pl.ds(base, sites), pl.ds(base + sites, sites)
            for s in range(nsite):
                part = slice(s * half, (s + 1) * half)
                areal = wreal[:, part] * scos + wimag[:, part] * ssin
                aimag = wreal[:, part] * ssin - wimag[:, part] * scos
                lhs[s, top, 0:half] = areal.astype(jnp.bfloat16)
                lhs[s, top, half : 2 * half] = aimag.astype(jnp.bfloat16)
                lhs[s, low, 0:half] = (-aimag).astype(jnp.bfloat16)
                lhs[s, low, half : 2 * half] = areal.astype(jnp.bfloat16)

    distances = list(range(nsite - 1, 0, -1))
    if nsite > 2:
        distances.remove(nsite // 2)
        distances.insert(0, nsite // 2)

    def partial_copy(group, distance):
        return pltpu.make_async_remote_copy(
            src_ref=outgoing[group].at[distance - 1],
            dst_ref=incoming[group].at[distance - 1],
            send_sem=psend_sem.at[group, distance - 1],
            recv_sem=precv_sem.at[group, distance - 1],
            device_id={"site": site_of(distance)},
            device_id_type=MESH,
        )

    def handle(group, block):
        for distance in distances:
            outgoing[group][distance - 1] = jnp.dot(
                block, lhs[site_of(distance)], preferred_element_type=jnp.float32
            ).astype(jnp.bfloat16)
            partial_copy(group, distance).start()
        own = jnp.dot(block, lhs[site], preferred_element_type=jnp.float32)
        for start, stop, column in places(group):
            total[column : column + stop - start, :] = own[start:stop]

    def places(group):
        if group == 0:
            return [(0, vrows, reach * vrows)]
        first, count = spans[group - 1]
        return [
            (i * count, (i + 1) * count, (o + reach) * vrows + first)
            for i, o in enumerate(offsets)
        ]

    def gather(group):
        for distance in distances:
            partial_copy(group, distance).wait_recv()
        for start, stop, column in places(group):
            value = total[column : column + stop - start, :]
            for distance in distances:
                value = value + incoming[group][distance - 1, start:stop].astype(jnp.float32)
            total[column : column + stop - start, :] = value

    handle(0, packed[...])
    for piece in range(npiece):
        for index in range(len(offsets)):
            vcopy(piece, index).wait_recv()
        handle(piece + 1, arrived[wide_spans[piece], :])
        gather(piece)
    gather(npiece)
    out_ref[...] = total[...].T
    for piece in range(npiece):
        for index in range(len(offsets)):
            vcopy(piece, index).wait_send()
    for group in range(npiece + 1):
        for distance in distances:
            partial_copy(group, distance).wait_send()


def shards(nmode, nsite, w_modes, v_modes, momenta):
    _, wrows, nsc, sites = w_modes.shape
    vrows = v_modes.shape[1]
    nph = momenta.shape[0]
    reach = min(REACH, (nmode - 1) // 2)
    nblocks = 2 * reach + 1
    rows = wrows // nsite
    width = 2 * nsc * sites
    lanes = 2 * nph * rows
    pieces = len(QUARTERS)
    out = pl.pallas_call(
        functools.partial(kernel, nmode, nsite, reach),
        out_shape=jax.ShapeDtypeStruct((lanes, nblocks * vrows), jnp.float32),
        in_specs=[
            pl.BlockSpec(memory_space=pltpu.HBM),
            pl.BlockSpec(memory_space=pltpu.HBM),
            pl.BlockSpec(memory_space=pltpu.HBM),
        ],
        out_specs=pl.BlockSpec(memory_space=pltpu.VMEM),
        scratch_shapes=[
            pltpu.VMEM((2, nsc, sites, wrows), jnp.bfloat16),
            pltpu.VMEM((2, nsc, vrows, sites), jnp.bfloat16),
            pltpu.SMEM((nph, 3), jnp.int32),
            pltpu.VMEM((vrows, width), jnp.bfloat16),
            pltpu.VMEM((2 * reach * vrows, width), jnp.bfloat16),
            pltpu.VMEM((nsite, width, lanes), jnp.bfloat16),
            pltpu.VMEM((nblocks * vrows, lanes), jnp.float32),
            pltpu.VMEM((nsite - 1, vrows, lanes), jnp.bfloat16),
            pltpu.VMEM((nsite - 1, 2 * reach * vrows, lanes), jnp.bfloat16),
            pltpu.VMEM((nsite - 1, vrows, lanes), jnp.bfloat16),
            pltpu.VMEM((nsite - 1, 2 * reach * vrows, lanes), jnp.bfloat16),
            pltpu.SemaphoreType.DMA((2 + pieces,)),
            pltpu.SemaphoreType.DMA((pieces, 2 * reach)),
            pltpu.SemaphoreType.DMA((pieces, 2 * reach)),
            pltpu.SemaphoreType.DMA((pieces + 1, nsite - 1)),
            pltpu.SemaphoreType.DMA((pieces + 1, nsite - 1)),
        ],
        compiler_params=pltpu.CompilerParams(
            collective_id=0, has_side_effects=True, vmem_limit_bytes=32 * 1024 * 1024
        ),
    )(
        pltpu.with_memory_space_constraint(jnp.transpose(w_modes, (0, 2, 3, 1)), pltpu.HBM),
        pltpu.with_memory_space_constraint(jnp.transpose(v_modes, (0, 2, 1, 3)), pltpu.HBM),
        pltpu.with_memory_space_constraint(momenta, pltpu.HBM),
    )
    return out.reshape(2, nph, rows, nblocks * vrows)


def solution(mesh):
    placed = (P(None, ("grp", "mode"), None, "site"), P(None, ("grp", "mode"), None, "site"), P())
    return jax.shard_map(
        functools.partial(shards, mesh.shape["mode"], mesh.shape["site"]),
        mesh=mesh,
        in_specs=placed,
        out_specs=P(None, None, ("grp", "mode", "site"), None),
        check_vma=False,
    )
```

```python
import functools

import jax
import jax.numpy as jnp
import numpy as np
from jax import lax
from jax.experimental import pallas as pl
from jax.experimental.pallas import tpu as pltpu
from jax.sharding import PartitionSpec as P

LAT = 96
REACH = 4
SPINS = 4
PIECES = 2
SIGNS = (-1.0, 1.0, 1.0, -1.0)
MESH = pl.DeviceIdType.MESH


def phase_table(mom_ref, nph, rows, sites):
    shape = (sites, nph * rows)
    index = lax.axis_index("site") * sites + lax.broadcasted_iota(jnp.int32, shape, 0)
    lane = lax.broadcasted_iota(jnp.int32, shape, 1)
    lat = jnp.full(shape, LAT, jnp.int32)
    xcoord = lax.rem(index, lat)
    upper = lax.div(index, lat)
    ycoord = lax.rem(upper, lat)
    zcoord = lax.div(upper, lat)
    total = jnp.zeros(shape, jnp.int32)
    for p in range(nph):
        here = mom_ref[p, 0] * xcoord + mom_ref[p, 1] * ycoord + mom_ref[p, 2] * zcoord
        total = jnp.where((lane >= p * rows) & (lane < (p + 1) * rows), here, total)
    wound = lax.rem(total, lat)
    wound = jnp.where(wound < 0, wound + LAT, wound)
    angle = (-2.0 * np.pi / LAT) * wound.astype(jnp.float32)
    return jnp.cos(angle), jnp.sin(angle)


def kernel(
    nmode, nsite, reach,
    w_hbm, v_hbm, mom_hbm, out_ref,
    w_ref, v_ref, mom_ref, packed, arrived, lhs, total,
    own_out, band_out, own_in, band_in,
    load_sem, vsend_sem, vrecv_sem, psend_sem, precv_sem,
):
    mode = lax.axis_index("mode")
    site = lax.axis_index("site")
    _, nsc, sites, wrows = w_ref.shape
    nph = mom_ref.shape[0]
    rows = wrows // nsite
    half = nph * rows
    npiece, prows, _ = packed.shape
    vrows = npiece * prows
    outgoing = [own_out] + [band_out.at[piece] for piece in range(npiece)]
    incoming = [own_in] + [band_in.at[piece] for piece in range(npiece)]
    step = 1 - 2 * lax.rem(site, 2) if nsite % 2 == 0 else 1

    def load_v(piece):
        return pltpu.make_async_copy(
            v_hbm.at[:, :, pl.ds(piece * prows, prows), :], v_ref.at[piece], load_sem.at[2 + piece]
        )

    for piece in range(npiece):
        load_v(piece).start()
    load_w = pltpu.make_async_copy(w_hbm, w_ref, load_sem.at[0])
    load_mom = pltpu.make_async_copy(mom_hbm, mom_ref, load_sem.at[1])
    load_mom.start()
    load_w.start()

    def mode_of(offset):
        return {"mode": lax.rem(mode + offset + nmode, nmode)}

    def site_of(distance):
        return lax.rem(site + step * distance + nsite, nsite)

    barrier = pltpu.get_barrier_semaphore()
    offsets = [o for o in range(-reach, reach + 1) if o != 0]
    for offset in offsets:
        pl.semaphore_signal(barrier, inc=1, device_id=mode_of(offset), device_id_type=MESH)
    for distance in range(1, nsite):
        pl.semaphore_signal(
            barrier, inc=1, device_id={"site": site_of(distance)}, device_id_type=MESH
        )

    def offset_at(index):
        return index - reach + jnp.where(index >= reach, 1, 0)

    def vcopy(piece, index):
        return pltpu.make_async_remote_copy(
            src_ref=packed.at[piece],
            dst_ref=arrived.at[piece, index],
            send_sem=vsend_sem.at[piece, index],
            recv_sem=vrecv_sem.at[piece, index],
            device_id=mode_of(-offset_at(index)),
            device_id_type=MESH,
        )

    if reach == 1 and npiece == 2:
        last = mode == nmode - 1
        end = (mode == 0) | last
        around = jnp.where(last, 0, 1)
        stages = [
            [(0, jnp.where(end, around, 0)), (jnp.where(end, 1, 0), jnp.where(end, around, 1))],
            [(jnp.where(end, 0, 1), jnp.where(end, 1 - around, 0)), (1, jnp.where(end, 1 - around, 1))],
        ]
    else:
        stages = [[(piece, index) for index in range(len(offsets))] for piece in range(npiece)]

    sends = [send for stage in stages for send in stage]
    for piece in range(npiece):
        load_v(piece).wait()
        for sc in range(nsc):
            packed[piece, :, sc * 2 * sites : (sc + 1) * 2 * sites] = jnp.concatenate(
                [v_ref[piece, 0, sc], v_ref[piece, 1, sc]], axis=1
            )
        if piece == 0:
            pl.semaphore_wait(barrier, len(offsets) + nsite - 1)
            vcopy(*sends[0]).start()
    for send in sends[1:]:
        vcopy(*send).start()

    load_mom.wait()
    cosine, sine = phase_table(mom_ref, nph, rows, sites)
    shape = (wrows, nsite * half)
    mode_row = lax.broadcasted_iota(jnp.int32, shape, 0)
    lane = lax.broadcasted_iota(jnp.int32, shape, 1)
    spread = jnp.zeros(shape, jnp.float32)
    for piece in range(nsite * nph):
        source = lane - piece * rows + (piece // nph) * rows
        inside = (lane >= piece * rows) & (lane < (piece + 1) * rows)
        spread = jnp.where(inside & (mode_row == source), 1.0, spread)
    spread = spread.astype(jnp.bfloat16)

    load_w.wait()
    colours = nsc // SPINS
    for spin in range(SPINS):
        taken = slice(colours * (SPINS - 1 - spin), colours * (SPINS - spin))
        both = jnp.concatenate(
            [w_ref[part, taken].reshape(colours * sites, wrows) for part in range(2)], axis=0
        )
        wide = jnp.dot(both, spread, preferred_element_type=jnp.float32)
        scos, ssin = SIGNS[spin] * cosine, SIGNS[spin] * sine
        for colour in range(colours):
            wreal = wide[colour * sites : (colour + 1) * sites]
            wimag = wide[(colours + colour) * sites : (colours + colour + 1) * sites]
            base = (colours * spin + colour) * 2 * sites
            top, low = pl.ds(base, sites), pl.ds(base + sites, sites)
            for s in range(nsite):
                part = slice(s * half, (s + 1) * half)
                areal = wreal[:, part] * scos + wimag[:, part] * ssin
                aimag = wreal[:, part] * ssin - wimag[:, part] * scos
                lhs[s, top, 0:half] = areal.astype(jnp.bfloat16)
                lhs[s, top, half : 2 * half] = aimag.astype(jnp.bfloat16)
                lhs[s, low, 0:half] = (-aimag).astype(jnp.bfloat16)
                lhs[s, low, half : 2 * half] = areal.astype(jnp.bfloat16)

    distances = list(range(nsite - 1, 0, -1))
    if nsite > 2:
        distances.remove(nsite // 2)
        distances.insert(0, nsite // 2)

    def partial_copy(group, distance):
        return pltpu.make_async_remote_copy(
            src_ref=outgoing[group].at[distance - 1],
            dst_ref=incoming[group].at[distance - 1],
            send_sem=psend_sem.at[group, distance - 1],
            recv_sem=precv_sem.at[group, distance - 1],
            device_id={"site": site_of(distance)},
            device_id_type=MESH,
        )

    def handle(group, block):
        for distance in distances:
            outgoing[group][distance - 1] = jnp.dot(
                block, lhs[site_of(distance)], preferred_element_type=jnp.float32
            ).astype(jnp.bfloat16)
            partial_copy(group, distance).start()
        own = jnp.dot(block, lhs[site], preferred_element_type=jnp.float32)
        for start, stop, column in places(group):
            total[column : column + stop - start, :] = own[start:stop]

    def places(group):
        if group == 0:
            return [(0, vrows, reach * vrows)]
        return [
            (i * prows, (i + 1) * prows, (o + reach) * vrows + (group - 1) * prows)
            for i, o in enumerate(offsets)
        ]

    def gather(group):
        for distance in distances:
            partial_copy(group, distance).wait_recv()
        for start, stop, column in places(group):
            value = total[column : column + stop - start, :]
            for distance in distances:
                value = value + incoming[group][distance - 1, start:stop].astype(jnp.float32)
            total[column : column + stop - start, :] = value

    handle(0, packed[...].reshape(vrows, -1))
    for piece in range(npiece):
        for index in range(len(offsets)):
            vcopy(piece, index).wait_recv()
        handle(piece + 1, arrived[piece].reshape(len(offsets) * prows, -1))
        gather(piece)
    gather(npiece)
    out_ref[...] = total[...].T
    for send in sends:
        vcopy(*send).wait_send()
    for group in range(npiece + 1):
        for distance in distances:
            partial_copy(group, distance).wait_send()


def shards(nmode, nsite, w_modes, v_modes, momenta):
    _, wrows, nsc, sites = w_modes.shape
    vrows = v_modes.shape[1]
    nph = momenta.shape[0]
    reach = min(REACH, (nmode - 1) // 2)
    nblocks = 2 * reach + 1
    rows = wrows // nsite
    width = 2 * nsc * sites
    lanes = 2 * nph * rows
    prows = vrows // PIECES
    out = pl.pallas_call(
        functools.partial(kernel, nmode, nsite, reach),
        out_shape=jax.ShapeDtypeStruct((lanes, nblocks * vrows), jnp.float32),
        in_specs=[
            pl.BlockSpec(memory_space=pltpu.HBM),
            pl.BlockSpec(memory_space=pltpu.HBM),
            pl.BlockSpec(memory_space=pltpu.HBM),
        ],
        out_specs=pl.BlockSpec(memory_space=pltpu.VMEM),
        scratch_shapes=[
            pltpu.VMEM((2, nsc, sites, wrows), jnp.bfloat16),
            pltpu.VMEM((PIECES, 2, nsc, prows, sites), jnp.bfloat16),
            pltpu.SMEM((nph, 3), jnp.int32),
            pltpu.VMEM((PIECES, prows, width), jnp.bfloat16),
            pltpu.VMEM((PIECES, 2 * reach, prows, width), jnp.bfloat16),
            pltpu.VMEM((nsite, width, lanes), jnp.bfloat16),
            pltpu.VMEM((nblocks * vrows, lanes), jnp.float32),
            pltpu.VMEM((nsite - 1, vrows, lanes), jnp.bfloat16),
            pltpu.VMEM((PIECES, nsite - 1, 2 * reach * prows, lanes), jnp.bfloat16),
            pltpu.VMEM((nsite - 1, vrows, lanes), jnp.bfloat16),
            pltpu.VMEM((PIECES, nsite - 1, 2 * reach * prows, lanes), jnp.bfloat16),
            pltpu.SemaphoreType.DMA((2 + PIECES,)),
            pltpu.SemaphoreType.DMA((PIECES, 2 * reach)),
            pltpu.SemaphoreType.DMA((PIECES, 2 * reach)),
            pltpu.SemaphoreType.DMA((PIECES + 1, nsite - 1)),
            pltpu.SemaphoreType.DMA((PIECES + 1, nsite - 1)),
        ],
        compiler_params=pltpu.CompilerParams(
            collective_id=0, has_side_effects=True, vmem_limit_bytes=32 * 1024 * 1024
        ),
    )(
        pltpu.with_memory_space_constraint(jnp.transpose(w_modes, (0, 2, 3, 1)), pltpu.HBM),
        pltpu.with_memory_space_constraint(jnp.transpose(v_modes, (0, 2, 1, 3)), pltpu.HBM),
        pltpu.with_memory_space_constraint(momenta, pltpu.HBM),
    )
    return out.reshape(2, nph, rows, nblocks * vrows)


def solution(mesh):
    placed = (P(None, ("grp", "mode"), None, "site"), P(None, ("grp", "mode"), None, "site"), P())
    return jax.shard_map(
        functools.partial(shards, mesh.shape["mode"], mesh.shape["site"]),
        mesh=mesh,
        in_specs=placed,
        out_specs=P(None, None, ("grp", "mode", "site"), None),
        check_vma=False,
    )
```

```python
import functools

import jax
import jax.numpy as jnp
import numpy as np
from jax import lax
from jax.experimental import pallas as pl
from jax.experimental.pallas import tpu as pltpu
from jax.sharding import PartitionSpec as P

LAT = 96
REACH = 4
SPINS = 4
PIECES = 1
SIGNS = (-1.0, 1.0, 1.0, -1.0)
MESH = pl.DeviceIdType.MESH


def phase_table(mom_ref, nph, rows, sites):
    shape = (sites, nph * rows)
    index = lax.axis_index("site") * sites + lax.broadcasted_iota(jnp.int32, shape, 0)
    lane = lax.broadcasted_iota(jnp.int32, shape, 1)
    lat = jnp.full(shape, LAT, jnp.int32)
    xcoord = lax.rem(index, lat)
    upper = lax.div(index, lat)
    ycoord = lax.rem(upper, lat)
    zcoord = lax.div(upper, lat)
    total = jnp.zeros(shape, jnp.int32)
    for p in range(nph):
        here = mom_ref[p, 0] * xcoord + mom_ref[p, 1] * ycoord + mom_ref[p, 2] * zcoord
        total = jnp.where((lane >= p * rows) & (lane < (p + 1) * rows), here, total)
    wound = lax.rem(total, lat)
    wound = jnp.where(wound < 0, wound + LAT, wound)
    angle = (-2.0 * np.pi / LAT) * wound.astype(jnp.float32)
    return jnp.cos(angle), jnp.sin(angle)


def kernel(
    nmode, nsite, reach,
    w_hbm, v_hbm, mom_hbm, out_ref,
    w_ref, v_ref, mom_ref, packed, arrived, lhs, total,
    own_out, band_out, own_in, band_in,
    load_sem, vsend_sem, vrecv_sem, psend_sem, precv_sem,
):
    mode = lax.axis_index("mode")
    site = lax.axis_index("site")
    _, nsc, sites, wrows = w_ref.shape
    nph = mom_ref.shape[0]
    rows = wrows // nsite
    half = nph * rows
    npiece, prows, _ = packed.shape
    vrows = npiece * prows
    outgoing = [own_out] + [band_out.at[piece] for piece in range(npiece)]
    incoming = [own_in] + [band_in.at[piece] for piece in range(npiece)]
    step = 1 - 2 * lax.rem(site, 2) if nsite % 2 == 0 else 1

    def load_v(piece):
        return pltpu.make_async_copy(
            v_hbm.at[:, :, pl.ds(piece * prows, prows), :], v_ref.at[piece], load_sem.at[2 + piece]
        )

    for piece in range(npiece):
        load_v(piece).start()
    load_w = pltpu.make_async_copy(w_hbm, w_ref, load_sem.at[0])
    load_mom = pltpu.make_async_copy(mom_hbm, mom_ref, load_sem.at[1])
    load_mom.start()
    load_w.start()

    def mode_of(offset):
        return {"mode": lax.rem(mode + offset + nmode, nmode)}

    def site_of(distance):
        return lax.rem(site + step * distance + nsite, nsite)

    barrier = pltpu.get_barrier_semaphore()
    offsets = [o for o in range(-reach, reach + 1) if o != 0]
    for offset in offsets:
        pl.semaphore_signal(barrier, inc=1, device_id=mode_of(offset), device_id_type=MESH)
    for distance in range(1, nsite):
        pl.semaphore_signal(
            barrier, inc=1, device_id={"site": site_of(distance)}, device_id_type=MESH
        )

    def offset_at(index):
        return index - reach + jnp.where(index >= reach, 1, 0)

    def vcopy(piece, index):
        return pltpu.make_async_remote_copy(
            src_ref=packed.at[piece],
            dst_ref=arrived.at[piece, index],
            send_sem=vsend_sem.at[piece, index],
            recv_sem=vrecv_sem.at[piece, index],
            device_id=mode_of(-offset_at(index)),
            device_id_type=MESH,
        )

    if reach == 1 and npiece == 2:
        last = mode == nmode - 1
        end = (mode == 0) | last
        around = jnp.where(last, 0, 1)
        stages = [
            [(0, jnp.where(end, around, 0)), (jnp.where(end, 1, 0), jnp.where(end, around, 1))],
            [(jnp.where(end, 0, 1), jnp.where(end, 1 - around, 0)), (1, jnp.where(end, 1 - around, 1))],
        ]
    else:
        stages = [[(piece, index) for index in range(len(offsets))] for piece in range(npiece)]

    sends = [send for stage in stages for send in stage]
    for piece in range(npiece):
        load_v(piece).wait()
        for sc in range(nsc):
            packed[piece, :, sc * 2 * sites : (sc + 1) * 2 * sites] = jnp.concatenate(
                [v_ref[piece, 0, sc], v_ref[piece, 1, sc]], axis=1
            )
        if piece == 0:
            pl.semaphore_wait(barrier, len(offsets) + nsite - 1)
            vcopy(*sends[0]).start()
    for send in sends[1:]:
        vcopy(*send).start()

    load_mom.wait()
    cosine, sine = phase_table(mom_ref, nph, rows, sites)
    shape = (wrows, nsite * half)
    mode_row = lax.broadcasted_iota(jnp.int32, shape, 0)
    lane = lax.broadcasted_iota(jnp.int32, shape, 1)
    spread = jnp.zeros(shape, jnp.float32)
    for piece in range(nsite * nph):
        source = lane - piece * rows + (piece // nph) * rows
        inside = (lane >= piece * rows) & (lane < (piece + 1) * rows)
        spread = jnp.where(inside & (mode_row == source), 1.0, spread)
    spread = spread.astype(jnp.bfloat16)

    load_w.wait()
    colours = nsc // SPINS
    for spin in range(SPINS):
        taken = slice(colours * (SPINS - 1 - spin), colours * (SPINS - spin))
        both = jnp.concatenate(
            [w_ref[part, taken].reshape(colours * sites, wrows) for part in range(2)], axis=0
        )
        wide = jnp.dot(both, spread, preferred_element_type=jnp.float32)
        scos, ssin = SIGNS[spin] * cosine, SIGNS[spin] * sine
        for colour in range(colours):
            wreal = wide[colour * sites : (colour + 1) * sites]
            wimag = wide[(colours + colour) * sites : (colours + colour + 1) * sites]
            base = (colours * spin + colour) * 2 * sites
            top, low = pl.ds(base, sites), pl.ds(base + sites, sites)
            for s in range(nsite):
                part = slice(s * half, (s + 1) * half)
                areal = wreal[:, part] * scos + wimag[:, part] * ssin
                aimag = wreal[:, part] * ssin - wimag[:, part] * scos
                lhs[s, top, 0:half] = areal.astype(jnp.bfloat16)
                lhs[s, top, half : 2 * half] = aimag.astype(jnp.bfloat16)
                lhs[s, low, 0:half] = (-aimag).astype(jnp.bfloat16)
                lhs[s, low, half : 2 * half] = areal.astype(jnp.bfloat16)

    distances = list(range(nsite - 1, 0, -1))
    if nsite > 2:
        distances.remove(nsite // 2)
        distances.insert(0, nsite // 2)

    def partial_copy(group, distance):
        return pltpu.make_async_remote_copy(
            src_ref=outgoing[group].at[distance - 1],
            dst_ref=incoming[group].at[distance - 1],
            send_sem=psend_sem.at[group, distance - 1],
            recv_sem=precv_sem.at[group, distance - 1],
            device_id={"site": site_of(distance)},
            device_id_type=MESH,
        )

    def handle(group, block):
        for distance in distances:
            outgoing[group][distance - 1] = jnp.dot(
                block, lhs[site_of(distance)], preferred_element_type=jnp.float32
            ).astype(jnp.bfloat16)
            partial_copy(group, distance).start()
        own = jnp.dot(block, lhs[site], preferred_element_type=jnp.float32)
        for start, stop, column in places(group):
            total[column : column + stop - start, :] = own[start:stop]

    def places(group):
        if group == 0:
            return [(0, vrows, reach * vrows)]
        return [
            (i * prows, (i + 1) * prows, (o + reach) * vrows + (group - 1) * prows)
            for i, o in enumerate(offsets)
        ]

    def gather(group):
        for distance in distances:
            partial_copy(group, distance).wait_recv()
        for start, stop, column in places(group):
            value = total[column : column + stop - start, :]
            for distance in distances:
                value = value + incoming[group][distance - 1, start:stop].astype(jnp.float32)
            total[column : column + stop - start, :] = value

    handle(0, packed[...].reshape(vrows, -1))
    for piece in range(npiece):
        for index in range(len(offsets)):
            vcopy(piece, index).wait_recv()
        handle(piece + 1, arrived[piece].reshape(len(offsets) * prows, -1))
        gather(piece)
    gather(npiece)
    out_ref[...] = total[...].T
    for send in sends:
        vcopy(*send).wait_send()
    for group in range(npiece + 1):
        for distance in distances:
            partial_copy(group, distance).wait_send()


def shards(nmode, nsite, w_modes, v_modes, momenta):
    _, wrows, nsc, sites = w_modes.shape
    vrows = v_modes.shape[1]
    nph = momenta.shape[0]
    reach = min(REACH, (nmode - 1) // 2)
    nblocks = 2 * reach + 1
    rows = wrows // nsite
    width = 2 * nsc * sites
    lanes = 2 * nph * rows
    prows = vrows // PIECES
    out = pl.pallas_call(
        functools.partial(kernel, nmode, nsite, reach),
        out_shape=jax.ShapeDtypeStruct((lanes, nblocks * vrows), jnp.float32),
        in_specs=[
            pl.BlockSpec(memory_space=pltpu.HBM),
            pl.BlockSpec(memory_space=pltpu.HBM),
            pl.BlockSpec(memory_space=pltpu.HBM),
        ],
        out_specs=pl.BlockSpec(memory_space=pltpu.VMEM),
        scratch_shapes=[
            pltpu.VMEM((2, nsc, sites, wrows), jnp.bfloat16),
            pltpu.VMEM((PIECES, 2, nsc, prows, sites), jnp.bfloat16),
            pltpu.SMEM((nph, 3), jnp.int32),
            pltpu.VMEM((PIECES, prows, width), jnp.bfloat16),
            pltpu.VMEM((PIECES, 2 * reach, prows, width), jnp.bfloat16),
            pltpu.VMEM((nsite, width, lanes), jnp.bfloat16),
            pltpu.VMEM((nblocks * vrows, lanes), jnp.float32),
            pltpu.VMEM((nsite - 1, vrows, lanes), jnp.bfloat16),
            pltpu.VMEM((PIECES, nsite - 1, 2 * reach * prows, lanes), jnp.bfloat16),
            pltpu.VMEM((nsite - 1, vrows, lanes), jnp.bfloat16),
            pltpu.VMEM((PIECES, nsite - 1, 2 * reach * prows, lanes), jnp.bfloat16),
            pltpu.SemaphoreType.DMA((2 + PIECES,)),
            pltpu.SemaphoreType.DMA((PIECES, 2 * reach)),
            pltpu.SemaphoreType.DMA((PIECES, 2 * reach)),
            pltpu.SemaphoreType.DMA((PIECES + 1, nsite - 1)),
            pltpu.SemaphoreType.DMA((PIECES + 1, nsite - 1)),
        ],
        compiler_params=pltpu.CompilerParams(
            collective_id=0, has_side_effects=True, vmem_limit_bytes=32 * 1024 * 1024
        ),
    )(
        pltpu.with_memory_space_constraint(jnp.transpose(w_modes, (0, 2, 3, 1)), pltpu.HBM),
        pltpu.with_memory_space_constraint(jnp.transpose(v_modes, (0, 2, 1, 3)), pltpu.HBM),
        pltpu.with_memory_space_constraint(momenta, pltpu.HBM),
    )
    return out.reshape(2, nph, rows, nblocks * vrows)


def solution(mesh):
    placed = (P(None, ("grp", "mode"), None, "site"), P(None, ("grp", "mode"), None, "site"), P())
    return jax.shard_map(
        functools.partial(shards, mesh.shape["mode"], mesh.shape["site"]),
        mesh=mesh,
        in_specs=placed,
        out_specs=P(None, None, ("grp", "mode", "site"), None),
        check_vma=False,
    )
```

```python
import functools

import jax
import jax.numpy as jnp
import numpy as np
from jax import lax
from jax.experimental import pallas as pl
from jax.experimental.pallas import tpu as pltpu
from jax.sharding import PartitionSpec as P

LAT = 96
REACH = 4
SPINS = 4
PIECES = 1
SIGNS = (-1.0, 1.0, 1.0, -1.0)
MESH = pl.DeviceIdType.MESH


def phase_table(mom_ref, nph, rows, sites):
    shape = (sites, nph * rows)
    index = lax.axis_index("site") * sites + lax.broadcasted_iota(jnp.int32, shape, 0)
    lane = lax.broadcasted_iota(jnp.int32, shape, 1)
    lat = jnp.full(shape, LAT, jnp.int32)
    xcoord = lax.rem(index, lat)
    upper = lax.div(index, lat)
    ycoord = lax.rem(upper, lat)
    zcoord = lax.div(upper, lat)
    total = jnp.zeros(shape, jnp.int32)
    for p in range(nph):
        here = mom_ref[p, 0] * xcoord + mom_ref[p, 1] * ycoord + mom_ref[p, 2] * zcoord
        total = jnp.where((lane >= p * rows) & (lane < (p + 1) * rows), here, total)
    wound = lax.rem(total, lat)
    wound = jnp.where(wound < 0, wound + LAT, wound)
    angle = (-2.0 * np.pi / LAT) * wound.astype(jnp.float32)
    return jnp.cos(angle), jnp.sin(angle)


def kernel(
    nmode, nsite, reach,
    w_hbm, v_hbm, mom_hbm, out_ref,
    w_ref, v_ref, mom_ref, packed, arrived, lhs, total,
    own_out, band_out, own_in, band_in,
    load_sem, vsend_sem, vrecv_sem, psend_sem, precv_sem,
):
    mode = lax.axis_index("mode")
    site = lax.axis_index("site")
    _, nsc, sites, wrows = w_ref.shape
    nph = mom_ref.shape[0]
    rows = wrows // nsite
    half = nph * rows
    npiece, prows, _ = packed.shape
    vrows = npiece * prows
    outgoing = [own_out] + [band_out.at[piece] for piece in range(npiece)]
    incoming = [own_in] + [band_in.at[piece] for piece in range(npiece)]
    step = 1 - 2 * lax.rem(site, 2) if nsite % 2 == 0 else 1

    def load_v(piece):
        return pltpu.make_async_copy(
            v_hbm.at[:, :, pl.ds(piece * prows, prows), :], v_ref.at[piece], load_sem.at[2 + piece]
        )

    for piece in range(npiece):
        load_v(piece).start()
    load_w = pltpu.make_async_copy(w_hbm, w_ref, load_sem.at[0])
    load_mom = pltpu.make_async_copy(mom_hbm, mom_ref, load_sem.at[1])
    load_mom.start()
    load_w.start()

    def mode_of(offset):
        return {"mode": lax.rem(mode + offset + nmode, nmode)}

    def site_of(distance):
        return lax.rem(site + step * distance + nsite, nsite)

    barrier = pltpu.get_barrier_semaphore()
    offsets = [o for o in range(-reach, reach + 1) if o != 0]
    for offset in offsets:
        pl.semaphore_signal(barrier, inc=1, device_id=mode_of(offset), device_id_type=MESH)
    for distance in range(1, nsite):
        pl.semaphore_signal(
            barrier, inc=1, device_id={"site": site_of(distance)}, device_id_type=MESH
        )

    def offset_at(index):
        return index - reach + jnp.where(index >= reach, 1, 0)

    def vcopy(piece, index):
        return pltpu.make_async_remote_copy(
            src_ref=packed.at[piece],
            dst_ref=arrived.at[piece, index],
            send_sem=vsend_sem.at[piece, index],
            recv_sem=vrecv_sem.at[piece, index],
            device_id=mode_of(-offset_at(index)),
            device_id_type=MESH,
        )

    if reach == 1 and npiece == 2:
        last = mode == nmode - 1
        end = (mode == 0) | last
        around = jnp.where(last, 0, 1)
        stages = [
            [(0, jnp.where(end, around, 0)), (jnp.where(end, 1, 0), jnp.where(end, around, 1))],
            [(jnp.where(end, 0, 1), jnp.where(end, 1 - around, 0)), (1, jnp.where(end, 1 - around, 1))],
        ]
    elif reach == 1 and npiece == 1:
        around = jnp.where(mode == nmode - 1, 0, 1)
        stages = [[(0, around), (0, 1 - around)]]
    else:
        stages = [[(piece, index) for index in range(len(offsets))] for piece in range(npiece)]

    sends = [send for stage in stages for send in stage]
    for piece in range(npiece):
        load_v(piece).wait()
        for sc in range(nsc):
            packed[piece, :, sc * 2 * sites : (sc + 1) * 2 * sites] = jnp.concatenate(
                [v_ref[piece, 0, sc], v_ref[piece, 1, sc]], axis=1
            )
        if piece == 0:
            pl.semaphore_wait(barrier, len(offsets) + nsite - 1)
            vcopy(*sends[0]).start()
    for send in sends[1:]:
        vcopy(*send).start()

    load_mom.wait()
    cosine, sine = phase_table(mom_ref, nph, rows, sites)
    shape = (wrows, nsite * half)
    mode_row = lax.broadcasted_iota(jnp.int32, shape, 0)
    lane = lax.broadcasted_iota(jnp.int32, shape, 1)
    spread = jnp.zeros(shape, jnp.float32)
    for piece in range(nsite * nph):
        source = lane - piece * rows + (piece // nph) * rows
        inside = (lane >= piece * rows) & (lane < (piece + 1) * rows)
        spread = jnp.where(inside & (mode_row == source), 1.0, spread)
    spread = spread.astype(jnp.bfloat16)

    load_w.wait()
    colours = nsc // SPINS
    for spin in range(SPINS):
        taken = slice(colours * (SPINS - 1 - spin), colours * (SPINS - spin))
        both = jnp.concatenate(
            [w_ref[part, taken].reshape(colours * sites, wrows) for part in range(2)], axis=0
        )
        wide = jnp.dot(both, spread, preferred_element_type=jnp.float32)
        scos, ssin = SIGNS[spin] * cosine, SIGNS[spin] * sine
        for colour in range(colours):
            wreal = wide[colour * sites : (colour + 1) * sites]
            wimag = wide[(colours + colour) * sites : (colours + colour + 1) * sites]
            base = (colours * spin + colour) * 2 * sites
            top, low = pl.ds(base, sites), pl.ds(base + sites, sites)
            for s in range(nsite):
                part = slice(s * half, (s + 1) * half)
                areal = wreal[:, part] * scos + wimag[:, part] * ssin
                aimag = wreal[:, part] * ssin - wimag[:, part] * scos
                lhs[s, top, 0:half] = areal.astype(jnp.bfloat16)
                lhs[s, top, half : 2 * half] = aimag.astype(jnp.bfloat16)
                lhs[s, low, 0:half] = (-aimag).astype(jnp.bfloat16)
                lhs[s, low, half : 2 * half] = areal.astype(jnp.bfloat16)

    distances = list(range(nsite - 1, 0, -1))
    if nsite > 2:
        distances.remove(nsite // 2)
        distances.insert(0, nsite // 2)

    def partial_copy(group, distance):
        return pltpu.make_async_remote_copy(
            src_ref=outgoing[group].at[distance - 1],
            dst_ref=incoming[group].at[distance - 1],
            send_sem=psend_sem.at[group, distance - 1],
            recv_sem=precv_sem.at[group, distance - 1],
            device_id={"site": site_of(distance)},
            device_id_type=MESH,
        )

    def handle(group, block):
        for distance in distances:
            outgoing[group][distance - 1] = jnp.dot(
                block, lhs[site_of(distance)], preferred_element_type=jnp.float32
            ).astype(jnp.bfloat16)
            partial_copy(group, distance).start()
        own = jnp.dot(block, lhs[site], preferred_element_type=jnp.float32)
        for start, stop, column in places(group):
            total[column : column + stop - start, :] = own[start:stop]

    def places(group):
        if group == 0:
            return [(0, vrows, reach * vrows)]
        return [
            (i * prows, (i + 1) * prows, (o + reach) * vrows + (group - 1) * prows)
            for i, o in enumerate(offsets)
        ]

    def gather(group):
        for distance in distances:
            partial_copy(group, distance).wait_recv()
        for start, stop, column in places(group):
            value = total[column : column + stop - start, :]
            for distance in distances:
                value = value + incoming[group][distance - 1, start:stop].astype(jnp.float32)
            total[column : column + stop - start, :] = value

    handle(0, packed[...].reshape(vrows, -1))
    for piece in range(npiece):
        for index in range(len(offsets)):
            vcopy(piece, index).wait_recv()
        handle(piece + 1, arrived[piece].reshape(len(offsets) * prows, -1))
        gather(piece)
    gather(npiece)
    out_ref[...] = total[...].T
    for send in sends:
        vcopy(*send).wait_send()
    for group in range(npiece + 1):
        for distance in distances:
            partial_copy(group, distance).wait_send()


def shards(nmode, nsite, w_modes, v_modes, momenta):
    _, wrows, nsc, sites = w_modes.shape
    vrows = v_modes.shape[1]
    nph = momenta.shape[0]
    reach = min(REACH, (nmode - 1) // 2)
    nblocks = 2 * reach + 1
    rows = wrows // nsite
    width = 2 * nsc * sites
    lanes = 2 * nph * rows
    prows = vrows // PIECES
    out = pl.pallas_call(
        functools.partial(kernel, nmode, nsite, reach),
        out_shape=jax.ShapeDtypeStruct((lanes, nblocks * vrows), jnp.float32),
        in_specs=[
            pl.BlockSpec(memory_space=pltpu.HBM),
            pl.BlockSpec(memory_space=pltpu.HBM),
            pl.BlockSpec(memory_space=pltpu.HBM),
        ],
        out_specs=pl.BlockSpec(memory_space=pltpu.VMEM),
        scratch_shapes=[
            pltpu.VMEM((2, nsc, sites, wrows), jnp.bfloat16),
            pltpu.VMEM((PIECES, 2, nsc, prows, sites), jnp.bfloat16),
            pltpu.SMEM((nph, 3), jnp.int32),
            pltpu.VMEM((PIECES, prows, width), jnp.bfloat16),
            pltpu.VMEM((PIECES, 2 * reach, prows, width), jnp.bfloat16),
            pltpu.VMEM((nsite, width, lanes), jnp.bfloat16),
            pltpu.VMEM((nblocks * vrows, lanes), jnp.float32),
            pltpu.VMEM((nsite - 1, vrows, lanes), jnp.bfloat16),
            pltpu.VMEM((PIECES, nsite - 1, 2 * reach * prows, lanes), jnp.bfloat16),
            pltpu.VMEM((nsite - 1, vrows, lanes), jnp.bfloat16),
            pltpu.VMEM((PIECES, nsite - 1, 2 * reach * prows, lanes), jnp.bfloat16),
            pltpu.SemaphoreType.DMA((2 + PIECES,)),
            pltpu.SemaphoreType.DMA((PIECES, 2 * reach)),
            pltpu.SemaphoreType.DMA((PIECES, 2 * reach)),
            pltpu.SemaphoreType.DMA((PIECES + 1, nsite - 1)),
            pltpu.SemaphoreType.DMA((PIECES + 1, nsite - 1)),
        ],
        compiler_params=pltpu.CompilerParams(
            collective_id=0, has_side_effects=True, vmem_limit_bytes=32 * 1024 * 1024
        ),
    )(
        pltpu.with_memory_space_constraint(jnp.transpose(w_modes, (0, 2, 3, 1)), pltpu.HBM),
        pltpu.with_memory_space_constraint(jnp.transpose(v_modes, (0, 2, 1, 3)), pltpu.HBM),
        pltpu.with_memory_space_constraint(momenta, pltpu.HBM),
    )
    return out.reshape(2, nph, rows, nblocks * vrows)


def solution(mesh):
    placed = (P(None, ("grp", "mode"), None, "site"), P(None, ("grp", "mode"), None, "site"), P())
    return jax.shard_map(
        functools.partial(shards, mesh.shape["mode"], mesh.shape["site"]),
        mesh=mesh,
        in_specs=placed,
        out_specs=P(None, None, ("grp", "mode", "site"), None),
        check_vma=False,
    )
```
